32 devices in a mesh: gx: 4 (over z), gy: 4 (over x, core), gz: 2 (over y).
Axes of the slice: x: 2, y: 2, z: 4, core: 2. Of those that a mesh axis runs over, the one named last changes fastest.
Arguments:
- field: float32 [256, 512, 512], P('gz', 'gx', 'gy'), may hold values from -6 to 6
- peaks: float32 [4], replicated, may hold values from -1.5 to 1.5
- tint: float32 [3], replicated, may hold values from -2 to 2
- light: float32 [3], replicated, may hold values from -1 to 1
Outputs:
- image: float32 [4, 512, 512], P(None, ('gx', 'gz'), 'gy')
The draws below stay inside these ranges and needn't reach their ends.
All inputs are finite; a program needn't handle non-finite values.
Results may differ from the reference program's by a relative error of at most 0.0003.
Values sent between devices are 32-bit elements; how exact they have to be, the bound alone decides.
No kernel may reach another device: no remote copies, remote signals or barrier semaphores. Data moves between devices by JAX's collectives and lax.ppermute only.
A program may use at most 256 MiB of HBM per device.

```python
import jax
import jax.numpy as jnp
from jax import lax

BUMPS = 4
NX = 512
NY = 512
NZ = 256


def shard_levels(own_key, dims, pieces, least, largest):
    def one(axis_at, blocks):
        draws = jax.random.uniform(jax.random.fold_in(jax.random.fold_in(own_key, 6), axis_at), (blocks,), jnp.float32, least / len(pieces), largest / len(pieces))
        return jnp.repeat(jnp.exp(draws), dims[axis_at] // blocks).reshape((-1,) + (1,) * (len(dims) - axis_at - 1))

    level = one(*pieces[0])
    for cut in pieces[1:]:
        level = level * one(*cut)
    return level


def bell_draw(rng, dims, deviation, limit, pieces=(), held_as=jnp.bfloat16):
    entries = jax.random.normal(rng, dims, jnp.float32) * deviation
    if len(pieces) > 0:
        entries = shard_levels(rng, dims, pieces, -0.22, 0.18) * entries
    return jnp.clip(entries, min=-limit, max=limit).astype(held_as)


def setup_inputs(seed: int = 0) -> dict:
    seeds = jax.random.split(jax.random.key(seed), 5)
    field = bell_draw(seeds[0], (NZ, NX, NY), 1.0, 6.0, ((0, 2), (1, 4), (2, 4)), jnp.float32)
    peaks = jnp.clip(jax.random.uniform(seeds[1], (BUMPS,), jnp.float32, -1.5, 1.5), -1.5, 1.5)
    tint = jnp.clip(jax.random.uniform(seeds[2], (3,), jnp.float32, -2.0, 2.0), -2.0, 2.0)
    light = jnp.clip(jax.random.uniform(seeds[3], (3,), jnp.float32, -1.0, 1.0), -1.0, 1.0)
    return dict(field=field, peaks=peaks, tint=tint, light=light)


extinction = 1.5

def shading(center, grad_x, grad_y, grad_z, peaks, tint, light, depth):
    bump = jnp.zeros_like(center)
    for index in range(peaks.shape[0]):
        bump = bump + jnp.exp(-2.0 * (center - peaks[index]) ** 2)
    tau = extinction / depth * bump
    inverse = lax.rsqrt(grad_x * grad_x + grad_y * grad_y + grad_z * grad_z + 1.0)
    shade = 0.3 + 0.7 * jnp.abs(grad_x * light[0] + grad_y * light[1] + grad_z * light[2]) * inverse
    colour = jnp.stack([jax.nn.sigmoid(tint[c] * center) * shade for c in range(3)])
    return (tau, colour)

def rolled_grad(center, axis):
    return (8.0 * (jnp.roll(center, -1, axis) - jnp.roll(center, 1, axis)) - (jnp.roll(center, -2, axis) - jnp.roll(center, 2, axis))) / 12.0

def reference(field, peaks, tint, light):
    if NX % 64 == 0:
        step_rows = 64
    else:
        step_rows = NX

    def one_block(block):
        rows = (block * step_rows + jnp.arange(step_rows + 4, dtype=jnp.int32) - 2) % NX
        slab = jnp.take(field, rows.astype(jnp.int32), axis=1)
        center = slab[:, 2:-2]
        grad_x = (8.0 * (slab[:, 3:-1] - slab[:, 1:-3]) - (slab[:, 4:] - slab[:, :-4])) / 12.0
        grad_y = rolled_grad(center, 2)
        grad_z = rolled_grad(center, 0)
        tau, colour = shading(center, grad_x, grad_y, grad_z, peaks, tint, light, NZ)
        optical = jnp.cumsum(tau, axis=0)
        weight = jnp.exp(tau - optical) * (1.0 - jnp.exp(-tau))
        colours = lax.optimization_barrier(jnp.sum(weight[None] * colour, axis=1))
        alpha = 1.0 - jnp.exp(-optical[-1])
        return jnp.concatenate([colours, alpha[None]], axis=0)
    blocks = lax.map(one_block, jnp.arange(NX // step_rows, dtype=jnp.int32))
    return jnp.transpose(blocks, (1, 0, 2, 3)).reshape(4, NX, NY)
```

```python
import functools
import math

import jax
import jax.numpy as jnp
from jax import lax
from jax.experimental import pallas as pl
from jax.experimental.pallas import tpu as pltpu
from jax.sharding import PartitionSpec as P

extinction = 1.5
LANES = 128
PAD = 8
HALO = 2
STEP = 16
GROUP = 32
AHEAD = 8
LOG2E = math.log2(math.e)
MIB = 1 << 20
F32 = jnp.float32
BF16 = jnp.bfloat16


def exchanged(first, last, axis):
    count = lax.axis_size(axis)
    forward = [(i, (i + 1) % count) for i in range(count)]
    backward = [(target, source) for source, target in forward]
    return lax.ppermute(last, axis, forward), lax.ppermute(first, axis, backward)


def exchanged_both(both, axis):
    count = lax.axis_size(axis)
    width = both.shape[0] // 2
    if count == 2:
        return lax.ppermute(both, axis, [(0, 1), (1, 0)]), width, 0
    return jnp.concatenate(exchanged(both[:width], both[width:], axis), axis=0), 0, width


def rows_of(shift, count, part):
    return pl.multiple_of(lax.rem(lax.axis_index("gz") + shift, count) * part, 8)


def weigh(peaks, scale, f, optical, before):
    bump = None
    for k in range(peaks.shape[0]):
        gap = f - peaks[k]
        term = jnp.exp2(gap * (gap * (-2.0 * LOG2E)))
        bump = term if bump is None else bump + term
    optical = optical + bump * scale
    after = jnp.exp2(optical)
    return optical, after, before - after


def pack_kernel(field, low, high, x_first, x_last, z_both, cells, totals, sems):
    depth, rows, _ = field.shape
    chunks = depth // STEP

    def fetch(chunk):
        at = pl.ds(chunk * STEP, STEP)
        return pltpu.make_async_copy(field.at[at], cells.at[at], sems.at[chunk])

    for chunk in range(chunks):
        fetch(chunk).start()
    lane = lax.broadcasted_iota(jnp.int32, (rows, LANES), 1)

    def one(block, none):
        offset = 2 + 2 * lax.rem(block, 2)
        group = (lane + (LANES + 2 - offset)) % LANES // 4
        total = jnp.zeros((rows, LANES), F32)
        for half in range(32 // STEP):
            chunk = block * (32 // STEP) + half
            fetch(chunk).wait()
            for step in range(STEP):
                z = chunk * STEP + step
                index = half * STEP + step
                total = jnp.where(group == index, pltpu.roll(cells[z], 4 * index + offset, 1), total)
                x_first[pl.ds(HALO * z, HALO), :] = cells[z, pl.ds(0, HALO), :]
                x_last[pl.ds(HALO * z, HALO), :] = cells[z, pl.ds(rows - HALO, HALO), :]
        totals[block] = total
        return none

    lax.fori_loop(0, depth // 32, one, 0)
    z_both[pl.ds(0, HALO)] = cells[pl.ds(0, HALO)]
    z_both[pl.ds(HALO, HALO)] = cells[pl.ds(depth - HALO, HALO)]
    odd = lane % 4 >= 2
    for block in range(depth // 64):
        one_half, two_half = totals[2 * block], totals[2 * block + 1]
        low[block] = jnp.where(odd, one_half, two_half)
        high[block] = jnp.where(odd, two_half, one_half)


def weight_kernel(scale, count, part, peaks, field, weight, through, cells, optical, sems):
    depth, _, _ = field.shape
    chunks = depth // STEP

    def fetch(turn, chunk):
        at = pl.ds(chunk * STEP, STEP)
        return pltpu.make_async_copy(
            field.at[at, pl.ds(rows_of(turn + 1, count, part), part), :],
            cells.at[at, pl.ds(turn * part, part), :],
            sems.at[turn, chunk],
        )

    for turn in range(count - 1):
        for chunk in range(chunks):
            fetch(turn, chunk).start()
    optical[...] = jnp.zeros_like(optical)
    through[...] = jnp.ones_like(through)
    for turn in range(count - 1):

        def one(chunk, none, turn=turn):
            fetch(turn, chunk).wait()
            depths, passed = optical[turn], through[turn]
            for step in range(STEP):
                z = chunk * STEP + step
                f = cells[z, pl.ds(turn * part, part), :]
                depths, passed, weight[turn, z] = weigh(peaks, scale, f, depths, passed)
            optical[turn], through[turn] = depths, passed
            return none

        lax.fori_loop(0, chunks, one, 0)


def edges(begin, part, low_halo, high_halo, low, high, edge):
    at = pl.ds(begin, part)
    place = lax.broadcasted_iota(jnp.int32, (part, LANES), 1) % 4
    for block in range(low.shape[0]):
        below = low_halo[block, at, :] - high[block, at, :]
        above = high_halo[block, at, :] - low[block, at, :]
        for half in range(2):
            if half == 1:
                below, above = pltpu.roll(below, LANES - 2, 1), pltpu.roll(above, LANES - 2, 1)
            right = jnp.where(place == 1, pltpu.roll(above, LANES - 1, 1), 0.0) - 0.125 * pltpu.roll(above, LANES - 2, 1)
            left = 0.125 * pltpu.roll(below, 2, 1) - jnp.where(place == 2, pltpu.roll(below, 1, 1), 0.0)
            edge[2 * block + half] = jnp.where(place < 2, right, left)


def difference_matrix():
    row = lax.broadcasted_iota(jnp.int32, (2 * LANES, LANES), 0)
    column = lax.broadcasted_iota(jnp.int32, (2 * LANES, LANES), 1)
    ahead = (row - column + 2 * LANES) % LANES
    values = jnp.where(ahead == 1, 1.0, jnp.where(ahead == LANES - 1, -1.0, 0.0))
    values = values + jnp.where(ahead == 2, -0.125, jnp.where(ahead == LANES - 2, 0.125, 0.0))
    return values.astype(BF16)


def shade_kernel(shift, count, part, group, ahead, lower_at, upper_at, scale, peaks, tint, light, field, weight, through,
                 x_low, x_high, z_both, low_halo, high_halo, low, high, out, cells, edge, matrix, slope_a, slope_b, sems):
    depth, rows, _ = field.shape
    chunks = depth // STEP
    begin = rows_of(shift, count, part)
    main = pl.ds(PAD, part)

    def fetch(chunk):
        at = pl.ds(chunk * STEP, STEP)
        into = pl.ds(HALO + chunk * STEP, STEP)
        below = pl.multiple_of(jnp.maximum(begin - PAD, 0), 8)
        above = pl.multiple_of(jnp.minimum(begin + part, rows - PAD), 8)
        return (
            pltpu.make_async_copy(field.at[at, pl.ds(begin, part), :], cells.at[into, main, :], sems.at[0, chunk]),
            pltpu.make_async_copy(field.at[at, pl.ds(below, PAD), :], cells.at[into, pl.ds(0, PAD), :], sems.at[1, chunk]),
            pltpu.make_async_copy(field.at[at, pl.ds(above, PAD), :], cells.at[into, pl.ds(PAD + part, PAD), :], sems.at[2, chunk]),
        )

    for chunk in range(chunks):
        for copy in fetch(chunk):
            copy.start()
    matrix[...] = difference_matrix()
    edges(begin, part, low_halo, high_halo, low, high, edge)
    cells[pl.ds(0, HALO), main, :] = z_both[pl.ds(lower_at, HALO), pl.ds(begin, part), :]
    cells[pl.ds(HALO + depth, HALO), main, :] = z_both[pl.ds(upper_at, HALO), pl.ds(begin, part), :]

    def arrive(chunk):
        for copy in fetch(chunk):
            copy.wait()

        @pl.when(begin == 0)
        def _():
            for step in range(STEP):
                z = chunk * STEP + step
                cells[HALO + z, pl.ds(PAD - HALO, HALO), :] = x_low[pl.ds(HALO * z, HALO), :]

        @pl.when(begin + part == rows)
        def _():
            for step in range(STEP):
                z = chunk * STEP + step
                cells[HALO + z, pl.ds(PAD + part, HALO), :] = x_high[pl.ds(HALO * z, HALO), :]

    arrive(0)
    lane = lax.broadcasted_iota(jnp.int32, (group, LANES), 1)
    rim = (lane < HALO) | (lane >= LANES - HALO)
    for start in range(0, part, group):

        def prepare(first, slopes):
            f = cells[pl.ds(HALO + first, ahead), pl.ds(PAD + start, group), :].reshape(ahead * group, LANES)
            upper = f.astype(BF16)
            lower = (f - upper.astype(F32)).astype(BF16)
            both = jnp.concatenate([upper, lower], axis=1)
            product = jnp.dot(both, matrix[...], preferred_element_type=F32)
            kept = edge[first // 32, pl.ds(start, group), :]
            for step in range(ahead):
                turn = lax.rem(2 * LANES - 2 - 4 * lax.rem(first + step, 32), LANES)
                fix = jnp.where(rim, pltpu.roll(kept, turn, 1), 0.0)
                slopes[step] = product[step * group : (step + 1) * group] + fix

        def use(first, slopes, carry):
            sums, seen = carry[:4], carry[4:]
            for step in range(ahead):
                z = first + step

                def at(dz, dx):
                    return cells[HALO + z + dz, PAD + start + dx : PAD + start + dx + group, :]

                def slope(far_up, up, down, far_down):
                    return (up - down) - 0.125 * (far_up - far_down)

                f = at(0, 0)
                qz = slope(at(2, 0), at(1, 0), at(-1, 0), at(-2, 0))
                qx = slope(at(0, 2), at(0, 1), at(0, -1), at(0, -2))
                qy = slopes[step]
                along = qx * (0.7 * light[0]) + qy * (0.7 * light[1]) + qz * (0.7 * light[2])
                inverse = lax.rsqrt(qx * qx + qy * qy + qz * qz + 2.25)
                if weight is None:
                    optical, passed, own = weigh(peaks, scale, f, *seen)
                    seen = (optical, passed)
                else:
                    own = weight[z, pl.ds(start, group), :]
                lit = own * (0.3 + jnp.abs(along * inverse))
                sums = (sums[0] + lit,) + tuple(
                    sums[c + 1] + lit * jnp.tanh(f * (0.5 * tint[c])) for c in range(3)
                )
            return sums + seen

        def one(chunk, carry):
            if start == 0:

                @pl.when(chunk + 1 < chunks)
                def _():
                    arrive(chunk + 1)

            for part_at in range(0, STEP, 2 * ahead):
                first = chunk * STEP + part_at
                prepare(first + ahead, slope_b)
                carry = use(first, slope_a, carry)
                prepare(jnp.minimum(first + 2 * ahead, depth - ahead), slope_a)
                carry = use(first + ahead, slope_b, carry)
            return carry

        prepare(0, slope_a)
        zero = jnp.zeros((group, LANES), F32)
        seen = (zero, zero + 1.0) if weight is None else ()
        carry = lax.fori_loop(0, chunks, one, (zero,) * 4 + seen)
        for c in range(3):
            out[c, pl.ds(start, group), :] = 0.5 * (carry[0] + carry[c + 1])
        out[3, pl.ds(start, group), :] = carry[5] if weight is None else through[pl.ds(start, group), :]


def fused_kernel(shift, count, part, group, ahead, lower_at, upper_at, scale, peaks, tint, light, field, *rest):
    shade_kernel(shift, count, part, group, ahead, lower_at, upper_at, scale, peaks, tint, light, field, None, None, *rest)


def blend_kernel(count, *refs):
    pieces, image = refs[:-1], refs[-1]
    me = lax.axis_index("gz")
    sources = [lax.rem(me + 2 * count - 1 - k, count) for k in range(count)]
    light = [piece[3] for piece in pieces]
    rgb = [None] * 3
    for k in range(count):
        before = jnp.ones_like(light[0])
        for other in range(count):
            if other != k:
                before = before * jnp.where(sources[other] < sources[k], light[other], 1.0)
        for c in range(3):
            term = before * pieces[k][c]
            rgb[c] = term if rgb[c] is None else rgb[c] + term
    for c in range(3):
        image[c] = rgb[c]
    image[3] = 1.0 - functools.reduce(jnp.multiply, light)


SMEM = pl.BlockSpec(memory_space=pltpu.SMEM)
VMEM = pl.BlockSpec(memory_space=pltpu.VMEM)
HBM = pl.BlockSpec(memory_space=pltpu.HBM)


def cost(cells, flops, terms):
    return pl.CostEstimate(flops=cells * flops, bytes_accessed=cells * 8, transcendentals=cells * terms)


def body(field, peaks, tint, light):
    depth, rows, lanes = field.shape
    count = lax.axis_size("gz")
    part = rows // count
    turns = count - 1
    cells = depth * rows * lanes
    chunks = depth // STEP
    shape = jax.ShapeDtypeStruct
    scale = -extinction / (depth * count) * LOG2E

    def params(mib):
        return pltpu.CompilerParams(vmem_limit_bytes=mib * MIB)

    low, high, x_first, x_last, z_own = pl.pallas_call(
        pack_kernel,
        out_shape=(
            shape((depth // 64, rows, lanes), F32),
            shape((depth // 64, rows, lanes), F32),
            shape((HALO * depth, lanes), F32),
            shape((HALO * depth, lanes), F32),
            shape((2 * HALO, rows, lanes), F32),
        ),
        in_specs=[HBM],
        out_specs=(VMEM,) * 5,
        scratch_shapes=[
            pltpu.VMEM((depth, rows, lanes), F32),
            pltpu.VMEM((depth // 32, rows, lanes), F32),
            pltpu.SemaphoreType.DMA((chunks,)),
        ],
        compiler_params=params(60),
        cost_estimate=cost(cells, 10, 0),
        name="pack",
    )(field)
    x_low, x_high = exchanged(x_first, x_last, "gx")
    z_both, lower_at, upper_at = exchanged_both(z_own, "gz")
    low_halo, high_halo = exchanged(low, high, "gy")

    weights, throughs = pl.pallas_call(
        functools.partial(weight_kernel, scale, count, part),
        out_shape=(pltpu.VMEM((turns, depth, part, lanes), F32), shape((turns, part, lanes), F32)),
        in_specs=[SMEM, HBM],
        out_specs=(VMEM, VMEM),
        scratch_shapes=[
            pltpu.VMEM((depth, turns * part, lanes), F32),
            pltpu.VMEM((turns, part, lanes), F32),
            pltpu.SemaphoreType.DMA((turns, chunks)),
        ],
        compiler_params=params(48),
        cost_estimate=cost(cells * turns // count, 18, 5),
        name="weights",
    )(peaks, field)

    group, ahead = min(GROUP, part), AHEAD
    pieces = []
    for turn in range(count):
        shift = (turn + 1) % count
        own = shift == 0
        operands = [peaks, tint, light, field]
        if not own:
            operands += [weights[turn], throughs[turn]]
        operands += [x_low, x_high, z_both, low_halo, high_halo, low, high]
        piece = pl.pallas_call(
            functools.partial(
                fused_kernel if own else shade_kernel, shift, count, part, group, ahead, lower_at, upper_at, scale
            ),
            out_shape=shape((4, part, lanes), F32),
            in_specs=[SMEM, SMEM, SMEM, HBM] + [VMEM] * (len(operands) - 4),
            out_specs=VMEM,
            scratch_shapes=[
                pltpu.VMEM((depth + 2 * HALO, part + 2 * PAD, lanes), F32),
                pltpu.VMEM((depth // 32, part, lanes), F32),
                pltpu.VMEM((2 * lanes, lanes), BF16),
                pltpu.VMEM((ahead, group, lanes), F32),
                pltpu.VMEM((ahead, group, lanes), F32),
                pltpu.SemaphoreType.DMA((3, chunks)),
            ],
            compiler_params=params(48),
            cost_estimate=cost(cells // count, 40, 4),
            name="fused" if own else "shade",
        )(*operands)
        if not own:
            piece = lax.ppermute(piece, "gz", [(i, (i + shift) % count) for i in range(count)])
        pieces.append(piece)
    return pl.pallas_call(
        functools.partial(blend_kernel, count),
        out_shape=shape((4, part, lanes), F32),
        in_specs=[VMEM] * count,
        out_specs=VMEM,
        name="blend",
    )(*pieces)


def solution(mesh):
    in_specs = (P("gz", "gx", "gy"), P(), P(), P())
    out_specs = P(None, ("gx", "gz"), "gy")
    return jax.shard_map(body, mesh=mesh, in_specs=in_specs, out_specs=out_specs, check_vma=False)
```

```python
import functools
import math

import jax
import jax.numpy as jnp
from jax import lax
from jax.experimental import pallas as pl
from jax.experimental.pallas import tpu as pltpu
from jax.sharding import PartitionSpec as P

extinction = 1.5
LANES = 128
PAD = 8
HALO = 2
STEP = 16
UNROLL = 16
GROUP = 64
AHEAD = 2
SLOTS = 4
WEIGHT_MIB = 44
SHADE_MIB = 36
FUSED_MIB = 48
LOG2E = math.log2(math.e)
MIB = 1 << 20
F32 = jnp.float32
BF16 = jnp.bfloat16


def exchanged(first, last, axis):
    count = lax.axis_size(axis)
    forward = [(i, (i + 1) % count) for i in range(count)]
    backward = [(target, source) for source, target in forward]
    return lax.ppermute(last, axis, forward), lax.ppermute(first, axis, backward)


def exchanged_both(both, axis):
    count = lax.axis_size(axis)
    width = both.shape[0] // 2
    if count == 2:
        return lax.ppermute(both, axis, [(0, 1), (1, 0)]), width, 0
    return jnp.concatenate(exchanged(both[:width], both[width:], axis), axis=0), 0, width


def rows_of(shift, count, part):
    return pl.multiple_of(lax.rem(lax.axis_index("gz") + shift, count) * part, 8)


def weigh(peaks, scale, f, optical, before):
    bump = None
    for k in range(peaks.shape[0]):
        gap = f - peaks[k]
        term = jnp.exp2(gap * (gap * (-2.0 * LOG2E)))
        bump = term if bump is None else bump + term
    optical = optical + bump * scale
    after = jnp.exp2(optical)
    return optical, after, before - after


def pack_kernel(field, low, high, x_first, x_last, z_both, cells, totals, sems):
    depth, rows, _ = field.shape
    chunks = depth // STEP

    def fetch(chunk):
        at = pl.ds(chunk * STEP, STEP)
        return pltpu.make_async_copy(field.at[at], cells.at[at], sems.at[chunk])

    for chunk in range(chunks):
        fetch(chunk).start()
    lane = lax.broadcasted_iota(jnp.int32, (rows, LANES), 1)

    def one(block, none):
        offset = 2 + 2 * lax.rem(block, 2)
        group = (lane + (LANES + 2 - offset)) % LANES // 4
        total = jnp.zeros((rows, LANES), F32)
        for half in range(32 // STEP):
            chunk = block * (32 // STEP) + half
            fetch(chunk).wait()
            for step in range(STEP):
                z = chunk * STEP + step
                index = half * STEP + step
                total = jnp.where(group == index, pltpu.roll(cells[z], 4 * index + offset, 1), total)
                x_first[pl.ds(HALO * z, HALO), :] = cells[z, pl.ds(0, HALO), :]
                x_last[pl.ds(HALO * z, HALO), :] = cells[z, pl.ds(rows - HALO, HALO), :]
        totals[block] = total
        return none

    lax.fori_loop(0, depth // 32, one, 0)
    for face in (x_first, x_last):
        face[pl.ds(HALO * depth, PAD), :] = jnp.zeros((PAD, LANES), F32)
    z_both[pl.ds(0, HALO)] = cells[pl.ds(0, HALO)]
    z_both[pl.ds(HALO, HALO)] = cells[pl.ds(depth - HALO, HALO)]
    odd = lane % 4 >= 2
    for block in range(depth // 64):
        one_half, two_half = totals[2 * block], totals[2 * block + 1]
        low[block] = jnp.where(odd, one_half, two_half)
        high[block] = jnp.where(odd, two_half, one_half)


def fetches(shift, count, part, field, cells, sems):
    _, rows, _ = field.shape
    begin = rows_of(shift, count, part)
    below = pl.multiple_of(jnp.maximum(begin - PAD, 0), 8)
    above = pl.multiple_of(jnp.minimum(begin + part, rows - PAD), 8)

    def fetch(chunk):
        at = pl.ds(chunk * STEP, STEP)
        into = pl.ds(HALO + chunk * STEP, STEP)
        return (
            pltpu.make_async_copy(field.at[at, pl.ds(begin, part), :], cells.at[into, pl.ds(PAD, part), :], sems.at[0, chunk]),
            pltpu.make_async_copy(field.at[at, pl.ds(below, PAD), :], cells.at[into, pl.ds(0, PAD), :], sems.at[1, chunk]),
            pltpu.make_async_copy(field.at[at, pl.ds(above, PAD), :], cells.at[into, pl.ds(PAD + part, PAD), :], sems.at[2, chunk]),
        )

    return fetch


def weight_kernel(scale, shift, count, part, peaks, field, weight, through, cells, optical, sems):
    depth, _, _ = field.shape
    chunks = depth // STEP
    fetch = fetches(shift, count, part, field, cells, sems)
    for chunk in range(chunks):
        for copy in fetch(chunk):
            copy.start()
    optical[...] = jnp.zeros_like(optical)
    through[...] = jnp.ones_like(through)

    def one(chunk, none):
        for ahead in range(1):
            for copy in fetch(chunk + ahead):
                copy.wait()
        depths, passed = optical[...], through[...]
        for step in range(STEP):
            z = chunk * STEP + step
            depths, passed, weight[z] = weigh(peaks, scale, cells[HALO + z, pl.ds(PAD, part), :], depths, passed)
        optical[...], through[...] = depths, passed
        return none

    lax.fori_loop(0, chunks, one, 0)


def split(f):
    upper = f.astype(BF16)
    return upper, (f - upper.astype(F32)).astype(BF16)


def edges(begin, part, low_halo, high_halo, low, high, edge):
    at = pl.ds(begin, part)
    place = lax.broadcasted_iota(jnp.int32, (part, LANES), 1) % 4
    for block in range(low.shape[0]):
        below = low_halo[block, at, :] - high[block, at, :]
        above = high_halo[block, at, :] - low[block, at, :]
        for half in range(2):
            if half == 1:
                below, above = pltpu.roll(below, LANES - 2, 1), pltpu.roll(above, LANES - 2, 1)
            right = jnp.where(place == 1, pltpu.roll(above, LANES - 1, 1), 0.0) - 0.125 * pltpu.roll(above, LANES - 2, 1)
            left = 0.125 * pltpu.roll(below, 2, 1) - jnp.where(place == 2, pltpu.roll(below, 1, 1), 0.0)
            edge[2 * block + half] = jnp.where(place < 2, right, left)


def slope_of(ahead):
    near = jnp.where(ahead == 1, 1.0, jnp.where(ahead == -1, -1.0, 0.0))
    return near + jnp.where(ahead == 2, -0.125, jnp.where(ahead == -2, 0.125, 0.0))


def lane_matrix():
    row = lax.broadcasted_iota(jnp.int32, (2 * LANES, LANES), 0)
    column = lax.broadcasted_iota(jnp.int32, (2 * LANES, LANES), 1)
    return slope_of((row - column + 2 * LANES + LANES // 2) % LANES - LANES // 2).astype(BF16)


def row_matrix(group):
    window = group + 2 * PAD
    row = lax.broadcasted_iota(jnp.int32, (group, window), 0)
    column = lax.broadcasted_iota(jnp.int32, (group, window), 1)
    slope = slope_of(column - PAD - row)
    return jnp.concatenate([slope, slope], axis=1).astype(BF16)


def shade_kernel(ready, shift, count, part, group, lower_at, upper_at, scale, peaks, tint, light, *refs):
    if ready:
        _, weight, through, *refs = refs
        (x_low, x_high, z_both, low_halo, high_halo, low, high, out, cells, edge, lanes, across, slopes) = refs
        depth = weight.shape[0]
    else:
        field, *refs = refs
        (x_low, x_high, z_both, low_halo, high_halo, low, high, out, cells, edge, lanes, across, slopes, sems) = refs
        depth = field.shape[0]
        fetch = fetches(shift, count, part, field, cells, sems)
    rows = z_both.shape[1]
    chunks = depth // STEP
    turns = depth // UNROLL
    begin = rows_of(shift, count, part)
    main = pl.ds(PAD, part)
    window = group + 2 * PAD

    if not ready:
        for chunk in range(chunks):
            for copy in fetch(chunk):
                copy.start()
    lanes[...] = lane_matrix()
    across[...] = row_matrix(group)
    edges(begin, part, low_halo, high_halo, low, high, edge)
    cells[pl.ds(0, HALO), main, :] = z_both[pl.ds(lower_at, HALO), pl.ds(begin, part), :]
    cells[pl.ds(HALO + depth, HALO), main, :] = z_both[pl.ds(upper_at, HALO), pl.ds(begin, part), :]

    def arrive(chunk, number):
        if not ready:
            for ahead in range(number):
                for copy in fetch(chunk + ahead):
                    copy.wait()

        @pl.when(begin == 0)
        def _():
            for step in range(number * STEP):
                z = chunk * STEP + step
                cells[HALO + z, pl.ds(PAD - HALO, HALO), :] = x_low[pl.ds(HALO * z, HALO), :]

        @pl.when(begin + part == rows)
        def _():
            for step in range(number * STEP):
                z = chunk * STEP + step
                cells[HALO + z, pl.ds(PAD + part, HALO), :] = x_high[pl.ds(HALO * z, HALO), :]

    arrive(0, UNROLL // STEP)
    lane = lax.broadcasted_iota(jnp.int32, (group, LANES), 1)
    rim = (lane < HALO) | (lane >= LANES - HALO)
    for start in range(0, part, group):

        def prepare(first, place):
            kept = edge[first // 32, pl.ds(start, group), :]
            halves = [split(cells[HALO + first + step, pl.ds(start, window), :]) for step in range(2)]
            rows_in = jnp.concatenate([jnp.concatenate(half, axis=1) for half in halves], axis=0)
            along_y = jnp.dot(rows_in, lanes[...], preferred_element_type=F32)
            both = [jnp.concatenate([halves[0][k], halves[1][k]], axis=1) for k in range(2)]
            along_x = jnp.dot(across[...], jnp.concatenate(both, axis=0), preferred_element_type=F32)
            for step in range(2):
                turn = lax.rem(2 * LANES - 2 - 4 * lax.rem(first + step, 32), LANES)
                fix = jnp.where(rim, pltpu.roll(kept, turn, 1), 0.0)
                slopes[(place + step) % SLOTS, 0] = along_x[:, step * LANES : (step + 1) * LANES]
                slopes[(place + step) % SLOTS, 1] = along_y[step * window + PAD : step * window + PAD + group] + fix

        def use(z, place, carry):
            sums, seen = carry[:4], carry[4:]

            def at(dz):
                return cells[HALO + z + dz, pl.ds(PAD + start, group), :]

            f = at(0)
            qx, qy = slopes[place % SLOTS, 0], slopes[place % SLOTS, 1]
            qz = (at(1) - at(-1)) - 0.125 * (at(2) - at(-2))
            along = qx * (0.7 * light[0]) + qy * (0.7 * light[1]) + qz * (0.7 * light[2])
            inverse = lax.rsqrt(qx * qx + qy * qy + qz * qz + 2.25)
            if ready:
                own = weight[z, pl.ds(start, group), :]
            else:
                optical, passed, own = weigh(peaks, scale, f, *seen)
                seen = (optical, passed)
            lit = own * (0.3 + jnp.abs(along * inverse))
            return (sums[0] + lit,) + tuple(sums[c + 1] + lit * jnp.tanh(f * (0.5 * tint[c])) for c in range(3)) + seen

        def one(turn, carry):
            if start == 0:

                @pl.when(turn + 1 < turns)
                def _():
                    arrive((turn + 1) * (UNROLL // STEP), UNROLL // STEP)

            for step in range(0, UNROLL, 2):
                z = turn * UNROLL + step
                later = z + AHEAD
                if step + AHEAD >= UNROLL:
                    later = jnp.minimum(later, depth - 4 + (AHEAD + step) % 4)
                prepare(later, step + AHEAD)
                carry = use(z, step, carry)
                carry = use(z + 1, step + 1, carry)
            return carry

        for step in range(0, AHEAD, 2):
            prepare(step, step)
        zero = jnp.zeros((group, LANES), F32)
        carry = lax.fori_loop(0, turns, one, (zero,) * 4 + (() if ready else (zero, zero + 1.0)))
        for c in range(3):
            out[c, pl.ds(start, group), :] = 0.5 * (carry[0] + carry[c + 1])
        out[3, pl.ds(start, group), :] = through[pl.ds(start, group), :] if ready else carry[5]


SMEM = pl.BlockSpec(memory_space=pltpu.SMEM)
VMEM = pl.BlockSpec(memory_space=pltpu.VMEM)
HBM = pl.BlockSpec(memory_space=pltpu.HBM)


def cost(cells, flops, terms):
    return pl.CostEstimate(flops=cells * flops, bytes_accessed=cells * 8, transcendentals=cells * terms)


def body(field, peaks, tint, light):
    depth, rows, lanes = field.shape
    count = lax.axis_size("gz")
    part = rows // count
    cells = depth * rows * lanes
    chunks = depth // STEP
    shape = jax.ShapeDtypeStruct
    scale = -extinction / (depth * count) * LOG2E

    def params(mib):
        return pltpu.CompilerParams(vmem_limit_bytes=mib * MIB)

    low, high, x_first, x_last, z_own = pl.pallas_call(
        pack_kernel,
        out_shape=(
            shape((depth // 64, rows, lanes), F32),
            shape((depth // 64, rows, lanes), F32),
            shape((HALO * depth + PAD, lanes), F32),
            shape((HALO * depth + PAD, lanes), F32),
            shape((2 * HALO, rows, lanes), F32),
        ),
        in_specs=[HBM],
        out_specs=(VMEM,) * 5,
        scratch_shapes=[
            pltpu.VMEM((depth, rows, lanes), F32),
            pltpu.VMEM((depth // 32, rows, lanes), F32),
            pltpu.SemaphoreType.DMA((chunks,)),
        ],
        compiler_params=params(48),
        cost_estimate=cost(cells, 10, 0),
        name="pack",
    )(field)
    x_low, x_high = exchanged(x_first, x_last, "gx")
    z_both, lower_at, upper_at = exchanged_both(z_own, "gz")
    low_halo, high_halo = exchanged(low, high, "gy")

    group = min(GROUP, part)
    padded = (depth + 2 * HALO, part + 2 * PAD, lanes)
    weight, through, ready_cells = pl.pallas_call(
        functools.partial(weight_kernel, scale, 1, count, part),
        out_shape=(pltpu.VMEM((depth, part, lanes), F32), shape((part, lanes), F32), pltpu.VMEM(padded, F32)),
        in_specs=[SMEM, HBM],
        out_specs=(VMEM, VMEM, VMEM),
        scratch_shapes=[pltpu.VMEM((part, lanes), F32), pltpu.SemaphoreType.DMA((3, chunks))],
        compiler_params=params(WEIGHT_MIB),
        cost_estimate=cost(cells // count, 18, 5),
        name="weights",
    )(peaks, field)

    pieces = []
    for turn in range(count):
        shift = (turn + 1) % count
        ready = turn == 0
        operands = [peaks, tint, light] + ([ready_cells, weight, through] if ready else [field])
        kinds = [SMEM] * 3 + ([VMEM] * 3 if ready else [HBM])
        halos = [x_low, x_high, z_both, low_halo, high_halo, low, high]
        scratch = [
            pltpu.VMEM((depth // 32, part, lanes), F32),
            pltpu.VMEM((2 * lanes, lanes), BF16),
            pltpu.VMEM((group, 2 * (group + 2 * PAD)), BF16),
            pltpu.VMEM((SLOTS, 2, group, lanes), F32),
        ]
        result = shape((4, part, lanes), F32)
        if not ready:
            scratch = [pltpu.VMEM(padded, F32)] + scratch + [pltpu.SemaphoreType.DMA((3, chunks))]
        piece = pl.pallas_call(
            functools.partial(shade_kernel, ready, shift, count, part, group, lower_at, upper_at, scale),
            out_shape=(result, pltpu.VMEM(padded, F32)) if ready else result,
            in_specs=kinds + [VMEM] * len(halos),
            out_specs=(VMEM, VMEM) if ready else VMEM,
            scratch_shapes=scratch,
            input_output_aliases={3: 1} if ready else {},
            compiler_params=params(SHADE_MIB if ready else FUSED_MIB),
            cost_estimate=cost(cells // count, 40, 4),
            name="shade" if ready else "fused",
        )(*operands, *halos)
        if ready:
            piece = piece[0]
        if shift:
            piece = lax.ppermute(piece, "gz", [(i, (i + shift) % count) for i in range(count)])
        pieces.append((lax.rem(lax.axis_index("gz") + count - shift, count), piece))

    image = 0.0
    for source, piece in pieces:
        for other, rest in pieces:
            if other is not source:
                piece = piece * jnp.where(other < source, rest[3:], 1.0)
        image = image + piece
    total = functools.reduce(jnp.multiply, [piece[3:] for _, piece in pieces])
    channel = lax.broadcasted_iota(jnp.int32, image.shape, 0)
    return jnp.where(channel < 3, image, 1.0 - total)


def solution(mesh):
    in_specs = (P("gz", "gx", "gy"), P(), P(), P())
    out_specs = P(None, ("gx", "gz"), "gy")
    return jax.shard_map(body, mesh=mesh, in_specs=in_specs, out_specs=out_specs, check_vma=False)
```

```python
import functools
import math

import jax
import jax.numpy as jnp
from jax import lax
from jax.experimental import pallas as pl
from jax.experimental.pallas import tpu as pltpu
from jax.sharding import PartitionSpec as P

extinction = 1.5
LANES = 128
PAD = 8
HALO = 2
STEP = 16
UNROLL = 32
GROUP = 64
AHEAD = 4
SLOTS = 8
QUAD = 4
WEIGHT_MIB = 24
SHADE_MIB = 24
FUSED_MIB = 48
LOG2E = math.log2(math.e)
MIB = 1 << 20
F32 = jnp.float32
BF16 = jnp.bfloat16


def exchanged(first, last, axis):
    count = lax.axis_size(axis)
    forward = [(i, (i + 1) % count) for i in range(count)]
    backward = [(target, source) for source, target in forward]
    return lax.ppermute(last, axis, forward), lax.ppermute(first, axis, backward)


def exchanged_both(both, axis):
    count = lax.axis_size(axis)
    width = both.shape[0] // 2
    if count == 2:
        return lax.ppermute(both, axis, [(0, 1), (1, 0)]), width, 0
    return jnp.concatenate(exchanged(both[:width], both[width:], axis), axis=0), 0, width


def rows_of(shift, count, part):
    return pl.multiple_of(lax.rem(lax.axis_index("gz") + shift, count) * part, 8)


def weigh(peaks, scale, f, optical, before):
    bump = None
    for k in range(peaks.shape[0]):
        gap = f - peaks[k]
        term = jnp.exp2(gap * (gap * (-2.0 * LOG2E)))
        bump = term if bump is None else bump + term
    optical = optical + bump * scale
    after = jnp.exp2(optical)
    return optical, after, before - after


def pack_kernel(field, low, high, x_first, x_last, z_both, cells, totals, sems):
    depth, rows, _ = field.shape
    chunks = depth // STEP

    def fetch(chunk):
        into = cells.at[pl.ds(HALO + chunk * STEP, STEP), pl.ds(PAD, rows), :]
        return pltpu.make_async_copy(field.at[pl.ds(chunk * STEP, STEP)], into, sems.at[chunk])

    for chunk in range(chunks):
        fetch(chunk).start()
    lane = lax.broadcasted_iota(jnp.int32, (rows, LANES), 1)

    def one(block, none):
        offset = 2 + 2 * lax.rem(block, 2)
        group = (lane + (LANES + 2 - offset)) % LANES // 4
        total = jnp.zeros((rows, LANES), F32)
        for half in range(32 // STEP):
            chunk = block * (32 // STEP) + half
            fetch(chunk).wait()
            for step in range(STEP):
                z = chunk * STEP + step
                index = half * STEP + step
                total = jnp.where(group == index, pltpu.roll(cells[HALO + z, pl.ds(PAD, rows), :], 4 * index + offset, 1), total)
                x_first[pl.ds(HALO * z, HALO), :] = cells[HALO + z, pl.ds(PAD, HALO), :]
                x_last[pl.ds(HALO * z, HALO), :] = cells[HALO + z, pl.ds(PAD + rows - HALO, HALO), :]
        totals[block] = total
        return none

    lax.fori_loop(0, depth // 32, one, 0)
    for face in (x_first, x_last):
        face[pl.ds(HALO * depth, PAD), :] = jnp.zeros((PAD, LANES), F32)
    z_both[pl.ds(0, HALO)] = cells[pl.ds(HALO, HALO), pl.ds(PAD, rows), :]
    z_both[pl.ds(HALO, HALO)] = cells[pl.ds(depth, HALO), pl.ds(PAD, rows), :]
    odd = lane % 4 >= 2
    for block in range(depth // 64):
        one_half, two_half = totals[2 * block], totals[2 * block + 1]
        low[block] = jnp.where(odd, one_half, two_half)
        high[block] = jnp.where(odd, two_half, one_half)


def weight_kernel(scale, shift, count, part, peaks, cells, weight, through, optical):
    depth = weight.shape[0]
    at = pl.ds(pl.multiple_of(rows_of(shift, count, part) + PAD, 8), part)
    optical[...] = jnp.zeros_like(optical)
    through[...] = jnp.ones_like(through)

    def one(turn, none):
        depths, passed = optical[...], through[...]
        for step in range(UNROLL):
            z = turn * UNROLL + step
            depths, passed, weight[z] = weigh(peaks, scale, cells[HALO + z, at, :], depths, passed)
        optical[...], through[...] = depths, passed
        return none

    lax.fori_loop(0, depth // UNROLL, one, 0)


def split(f):
    upper = f.astype(BF16)
    return upper, (f - upper.astype(F32)).astype(BF16)


def edges(begin, part, low_halo, high_halo, low, high, edge):
    at = pl.ds(begin, part)
    place = lax.broadcasted_iota(jnp.int32, (part, LANES), 1) % 4
    for block in range(low.shape[0]):
        below = low_halo[block, at, :] - high[block, at, :]
        above = high_halo[block, at, :] - low[block, at, :]
        for half in range(2):
            if half == 1:
                below, above = pltpu.roll(below, LANES - 2, 1), pltpu.roll(above, LANES - 2, 1)
            right = jnp.where(place == 1, pltpu.roll(above, LANES - 1, 1), 0.0) - 0.125 * pltpu.roll(above, LANES - 2, 1)
            left = 0.125 * pltpu.roll(below, 2, 1) - jnp.where(place == 2, pltpu.roll(below, 1, 1), 0.0)
            edge[2 * block + half] = jnp.where(place < 2, right, left)


def slope_of(ahead):
    near = jnp.where(ahead == 1, 1.0, jnp.where(ahead == -1, -1.0, 0.0))
    return near + jnp.where(ahead == 2, -0.125, jnp.where(ahead == -2, 0.125, 0.0))


def lane_matrix():
    row = lax.broadcasted_iota(jnp.int32, (2 * LANES, LANES), 0)
    column = lax.broadcasted_iota(jnp.int32, (2 * LANES, LANES), 1)
    return slope_of((row - column + 2 * LANES + LANES // 2) % LANES - LANES // 2).astype(BF16)


def row_matrix(group):
    width = group + 2 * PAD
    row = lax.broadcasted_iota(jnp.int32, (group, width), 0)
    column = lax.broadcasted_iota(jnp.int32, (group, width), 1)
    cell = jnp.where(column < group, column, jnp.where(column < group + PAD, column - group - PAD, column - PAD))
    slope = slope_of(cell - row)
    return jnp.concatenate([slope, slope], axis=1).astype(BF16)


def shade_kernel(shift, count, part, group, lower_at, upper_at, scale, peaks, tint, light, *refs):
    cells, weight, through, *refs = refs
    x_low, x_high, z_both, low_halo, high_halo, low, high, out, edge, lanes, across, slopes, strips = refs
    depth, rows = cells.shape[0] - 2 * HALO, low.shape[1]
    turns = depth // UNROLL
    begin = rows_of(shift, count, part)
    lowest, highest = begin == 0, begin + part == rows

    def beside(turn, none):
        for step in range(UNROLL):
            plane = cells.at[HALO + turn * UNROLL + step]
            below, above = plane[pl.ds(begin, PAD), :], plane[pl.ds(pl.multiple_of(begin + PAD + part, 8), PAD), :]
            strips[turn * UNROLL + step, pl.ds(0, PAD), :] = jnp.where(lowest, 0.0, below)
            strips[turn * UNROLL + step, pl.ds(PAD, PAD), :] = jnp.where(highest, 0.0, above)
        return none

    def beside_halo(turn, none, row, halo):
        for step in range(UNROLL):
            z = turn * UNROLL + step
            strips[z, pl.ds(row, HALO), :] = halo[pl.ds(HALO * z, HALO), :]
        return none

    lax.fori_loop(0, turns, beside, 0)

    @pl.when(lowest)
    def _():
        lax.fori_loop(0, turns, functools.partial(beside_halo, row=PAD - HALO, halo=x_low), 0)

    @pl.when(highest)
    def _():
        lax.fori_loop(0, turns, functools.partial(beside_halo, row=PAD, halo=x_high), 0)

    lanes[...] = lane_matrix()
    across[...] = row_matrix(group)
    edges(begin, part, low_halo, high_halo, low, high, edge)
    lane = lax.broadcasted_iota(jnp.int32, (group, LANES), 1)
    rim = (lane < HALO) | (lane >= LANES - HALO)
    for start in range(0, part, group):
        row = pl.multiple_of(begin + start, 8)

        def halved(first, number):
            inner, outer = [], []
            for step in range(number):
                plane = cells.at[HALO + first + step]
                inner.append(split(plane[pl.ds(pl.multiple_of(row + PAD, 8), group), :]))
                below = strips[first + step, pl.ds(0, PAD), :] if start == 0 else plane[pl.ds(row, PAD), :]
                if start + group == part:
                    above = strips[first + step, pl.ds(PAD, PAD), :]
                else:
                    above = plane[pl.ds(pl.multiple_of(row + PAD + group, 8), PAD), :]
                outer.append(split(jnp.concatenate([below, above], axis=0)))
            return inner, outer

        def prepare(first, place):
            kept = edge[first // 32, pl.ds(start, group), :]
            halves, sides = halved(first, QUAD)
            rows_in = jnp.concatenate([jnp.concatenate(half, axis=1) for half in halves], axis=0)
            along_y = jnp.dot(rows_in, lanes[...], preferred_element_type=F32)[:, :LANES]
            for step in range(QUAD):
                turn = lax.rem(2 * LANES - 2 - 4 * lax.rem(first + step, 32), LANES)
                fix = jnp.where(rim, pltpu.roll(kept, turn, 1), 0.0)
                slopes[(place + step) % SLOTS, 1] = along_y[step * group : (step + 1) * group] + fix
            for pair in range(0, QUAD, 2):
                both = [
                    jnp.concatenate([rows[pair][k], rows[pair + 1][k]], axis=1) for k in range(2) for rows in (halves, sides)
                ]
                along_x = jnp.dot(across[...], jnp.concatenate(both, axis=0), preferred_element_type=F32)
                for step in range(2):
                    slopes[(place + pair + step) % SLOTS, 0] = along_x[:, step * LANES : (step + 1) * LANES]

        def use(turn, step, carry):
            z, place = turn * UNROLL + step, step
            sums = carry

            def at(dz):
                layer = cells[HALO + z + dz, pl.ds(pl.multiple_of(row + PAD, 8), group), :]
                if step + dz < 0:
                    layer = jnp.where(turn == 0, z_both[lower_at + HALO + step + dz, pl.ds(row, group), :], layer)
                if step + dz >= UNROLL:
                    beyond = z_both[upper_at + step + dz - UNROLL, pl.ds(row, group), :]
                    layer = jnp.where(turn == turns - 1, beyond, layer)
                return layer

            f = at(0)
            qx, qy = slopes[place % SLOTS, 0], slopes[place % SLOTS, 1]
            qz = (at(1) - at(-1)) - 0.125 * (at(2) - at(-2))
            along = qx * (0.7 * light[0]) + qy * (0.7 * light[1]) + qz * (0.7 * light[2])
            inverse = lax.rsqrt(qx * qx + qy * qy + qz * qz + 2.25)
            own = weight[z, pl.ds(start, group), :]
            lit = own * (0.3 + jnp.abs(along * inverse))
            return (sums[0] + lit,) + tuple(sums[c + 1] + lit * jnp.tanh(f * (0.5 * tint[c])) for c in range(3))

        def one(turn, carry):
            for step in range(0, UNROLL, QUAD):
                z = turn * UNROLL + step
                later = z + AHEAD
                if step + AHEAD >= UNROLL:
                    later = jnp.minimum(later, depth - QUAD)
                prepare(later, step + AHEAD)
                for near in range(QUAD):
                    carry = use(turn, step + near, carry)
            return carry

        for step in range(0, AHEAD, QUAD):
            prepare(step, step)
        zero = jnp.zeros((group, LANES), F32)
        carry = lax.fori_loop(0, turns, one, (zero,) * 4)
        for c in range(3):
            out[c, pl.ds(start, group), :] = 0.5 * (carry[0] + carry[c + 1])
        out[3, pl.ds(start, group), :] = through[pl.ds(start, group), :]


def fetches(shift, count, part, field, cells, sems):
    _, rows, _ = field.shape
    begin = rows_of(shift, count, part)
    below = pl.multiple_of(jnp.maximum(begin - PAD, 0), 8)
    above = pl.multiple_of(jnp.minimum(begin + part, rows - PAD), 8)

    def fetch(chunk):
        at = pl.ds(chunk * STEP, STEP)
        into = pl.ds(HALO + chunk * STEP, STEP)
        return (
            pltpu.make_async_copy(field.at[at, pl.ds(begin, part), :], cells.at[into, pl.ds(PAD, part), :], sems.at[0, chunk]),
            pltpu.make_async_copy(field.at[at, pl.ds(below, PAD), :], cells.at[into, pl.ds(0, PAD), :], sems.at[1, chunk]),
            pltpu.make_async_copy(field.at[at, pl.ds(above, PAD), :], cells.at[into, pl.ds(PAD + part, PAD), :], sems.at[2, chunk]),
        )

    return fetch


def fused_kernel(shift, count, part, group, lower_at, upper_at, scale, peaks, tint, light, *refs):
    field, *refs = refs
    x_low, x_high, z_both, low_halo, high_halo, low, high, out, cells, edge, lanes, across, slopes, sems = refs
    depth = field.shape[0]
    fetch = fetches(shift, count, part, field, cells, sems)
    rows = z_both.shape[1]
    chunks = depth // STEP
    turns = depth // UNROLL
    begin = rows_of(shift, count, part)
    main = pl.ds(PAD, part)

    for chunk in range(chunks):
        for copy in fetch(chunk):
            copy.start()
    lanes[...] = lane_matrix()
    across[...] = row_matrix(group)
    edges(begin, part, low_halo, high_halo, low, high, edge)
    cells[pl.ds(0, HALO), main, :] = z_both[pl.ds(lower_at, HALO), pl.ds(begin, part), :]
    cells[pl.ds(HALO + depth, HALO), main, :] = z_both[pl.ds(upper_at, HALO), pl.ds(begin, part), :]

    def beside(first, number):
        @pl.when(begin == 0)
        def _():
            for step in range(number):
                cells[HALO + first + step, pl.ds(PAD - HALO, HALO), :] = x_low[pl.ds(HALO * (first + step), HALO), :]

        @pl.when(begin + part == rows)
        def _():
            for step in range(number):
                cells[HALO + first + step, pl.ds(PAD + part, HALO), :] = x_high[pl.ds(HALO * (first + step), HALO), :]

    def arrive(chunk, number):
        for ahead in range(number):
            for copy in fetch(chunk + ahead):
                copy.wait()
        beside(chunk * STEP, number * STEP)

    arrive(0, 1)
    lane = lax.broadcasted_iota(jnp.int32, (group, LANES), 1)
    rim = (lane < HALO) | (lane >= LANES - HALO)
    for start in range(0, part, group):

        def halved(first, number):
            inner, outer = [], []
            for step in range(number):
                plane = cells.at[HALO + first + step]
                inner.append(split(plane[pl.ds(PAD + start, group), :]))
                below, above = plane[pl.ds(start, PAD), :], plane[pl.ds(PAD + start + group, PAD), :]
                outer.append(split(jnp.concatenate([below, above], axis=0)))
            return inner, outer

        def prepare(first, place):
            kept = edge[first // 32, pl.ds(start, group), :]
            halves, sides = halved(first, QUAD)
            rows_in = jnp.concatenate([jnp.concatenate(half, axis=1) for half in halves], axis=0)
            along_y = jnp.dot(rows_in, lanes[...], preferred_element_type=F32)[:, :LANES]
            for step in range(QUAD):
                turn = lax.rem(2 * LANES - 2 - 4 * lax.rem(first + step, 32), LANES)
                fix = jnp.where(rim, pltpu.roll(kept, turn, 1), 0.0)
                slopes[(place + step) % SLOTS, 1] = along_y[step * group : (step + 1) * group] + fix
            for pair in range(0, QUAD, 2):
                both = [
                    jnp.concatenate([rows[pair][k], rows[pair + 1][k]], axis=1) for k in range(2) for rows in (halves, sides)
                ]
                along_x = jnp.dot(across[...], jnp.concatenate(both, axis=0), preferred_element_type=F32)
                for step in range(2):
                    slopes[(place + pair + step) % SLOTS, 0] = along_x[:, step * LANES : (step + 1) * LANES]

        def use(z, place, carry):
            sums, seen = carry[:4], carry[4:]

            def at(dz):
                return cells[HALO + z + dz, pl.ds(PAD + start, group), :]

            f = at(0)
            qx, qy = slopes[place % SLOTS, 0], slopes[place % SLOTS, 1]
            qz = (at(1) - at(-1)) - 0.125 * (at(2) - at(-2))
            along = qx * (0.7 * light[0]) + qy * (0.7 * light[1]) + qz * (0.7 * light[2])
            inverse = lax.rsqrt(qx * qx + qy * qy + qz * qz + 2.25)
            optical, passed, own = weigh(peaks, scale, f, *seen)
            seen = (optical, passed)
            lit = own * (0.3 + jnp.abs(along * inverse))
            return (sums[0] + lit,) + tuple(sums[c + 1] + lit * jnp.tanh(f * (0.5 * tint[c])) for c in range(3)) + seen

        def one(turn, carry):
            if start == 0:
                chunk = turn * (UNROLL // STEP) + 1

                @pl.when(turn + 1 < turns)
                def _():
                    arrive(chunk, UNROLL // STEP)

                @pl.when(turn + 1 == turns)
                def _():
                    arrive(chunk, UNROLL // STEP - 1)

            for step in range(0, UNROLL, QUAD):
                z = turn * UNROLL + step
                later = z + AHEAD
                if step + AHEAD >= UNROLL:
                    later = jnp.minimum(later, depth - QUAD)
                prepare(later, step + AHEAD)
                for near in range(QUAD):
                    carry = use(z + near, step + near, carry)
            return carry

        for step in range(0, AHEAD, QUAD):
            prepare(step, step)
        zero = jnp.zeros((group, LANES), F32)
        carry = lax.fori_loop(0, turns, one, (zero,) * 5 + (zero + 1.0,))
        for c in range(3):
            out[c, pl.ds(start, group), :] = 0.5 * (carry[0] + carry[c + 1])
        out[3, pl.ds(start, group), :] = carry[5]


SMEM = pl.BlockSpec(memory_space=pltpu.SMEM)
VMEM = pl.BlockSpec(memory_space=pltpu.VMEM)
HBM = pl.BlockSpec(memory_space=pltpu.HBM)


def cost(cells, flops, terms):
    return pl.CostEstimate(flops=cells * flops, bytes_accessed=cells * 8, transcendentals=cells * terms)


def body(field, peaks, tint, light):
    depth, rows, lanes = field.shape
    count = lax.axis_size("gz")
    part = rows // count
    cells = depth * rows * lanes
    chunks = depth // STEP
    shape = jax.ShapeDtypeStruct
    scale = -extinction / (depth * count) * LOG2E

    def params(mib):
        return pltpu.CompilerParams(vmem_limit_bytes=mib * MIB)

    padded = (depth + 2 * HALO, rows + 2 * PAD, lanes)
    low, high, x_first, x_last, z_own, cells_in = pl.pallas_call(
        pack_kernel,
        out_shape=(
            shape((depth // 64, rows, lanes), F32),
            shape((depth // 64, rows, lanes), F32),
            shape((HALO * depth + PAD, lanes), F32),
            shape((HALO * depth + PAD, lanes), F32),
            shape((2 * HALO, rows, lanes), F32),
            pltpu.VMEM(padded, F32),
        ),
        in_specs=[HBM],
        out_specs=(VMEM,) * 6,
        scratch_shapes=[
            pltpu.VMEM((depth // 32, rows, lanes), F32),
            pltpu.SemaphoreType.DMA((chunks,)),
        ],
        compiler_params=params(48),
        cost_estimate=cost(cells, 10, 0),
        name="pack",
    )(field)
    x_low, x_high = exchanged(x_first, x_last, "gx")
    z_both, lower_at, upper_at = exchanged_both(z_own, "gz")
    low_halo, high_halo = exchanged(low, high, "gy")

    group = min(GROUP, part)
    weight, through = pl.pallas_call(
        functools.partial(weight_kernel, scale, 1, count, part),
        out_shape=(pltpu.VMEM((depth, part, lanes), F32), shape((part, lanes), F32)),
        in_specs=[SMEM, VMEM],
        out_specs=(VMEM, VMEM),
        scratch_shapes=[pltpu.VMEM((part, lanes), F32)],
        compiler_params=params(WEIGHT_MIB),
        cost_estimate=cost(cells // count, 18, 5),
        name="weights",
    )(peaks, cells_in)

    pieces = []
    for turn in range(count):
        shift = (turn + 1) % count
        ready = turn == 0
        operands = [peaks, tint, light] + ([cells_in, weight, through] if ready else [field])
        halos = [x_low, x_high, z_both, low_halo, high_halo, low, high]
        scratch = [
            pltpu.VMEM((depth // 32, part, lanes), F32),
            pltpu.VMEM((2 * lanes, lanes), BF16),
            pltpu.VMEM((group, 2 * (group + 2 * PAD)), BF16),
            pltpu.VMEM((SLOTS, 2, group, lanes), F32),
        ]
        if ready:
            scratch.append(pltpu.VMEM((depth, 2 * PAD, lanes), F32))
        else:
            own_cells = pltpu.VMEM((depth + 2 * HALO, part + 2 * PAD, lanes), F32)
            scratch = [own_cells] + scratch + [pltpu.SemaphoreType.DMA((3, chunks))]
        result = shape((4, part, lanes), F32)
        piece = pl.pallas_call(
            functools.partial(shade_kernel if ready else fused_kernel, shift, count, part, group, lower_at, upper_at, scale),
            out_shape=result,
            in_specs=[SMEM] * 3 + ([VMEM] * 3 if ready else [HBM]) + [VMEM] * len(halos),
            out_specs=VMEM,
            scratch_shapes=scratch,
            compiler_params=params(SHADE_MIB if ready else FUSED_MIB),
            cost_estimate=cost(cells // count, 40, 4),
            name="shade" if ready else "fused",
        )(*operands, *halos)
        if shift:
            piece = lax.ppermute(piece, "gz", [(i, (i + shift) % count) for i in range(count)])
        pieces.append((lax.rem(lax.axis_index("gz") + count - shift, count), piece))

    image = 0.0
    for source, piece in pieces:
        for other, rest in pieces:
            if other is not source:
                piece = piece * jnp.where(other < source, rest[3:], 1.0)
        image = image + piece
    total = functools.reduce(jnp.multiply, [piece[3:] for _, piece in pieces])
    channel = lax.broadcasted_iota(jnp.int32, image.shape, 0)
    return jnp.where(channel < 3, image, 1.0 - total)


def solution(mesh):
    in_specs = (P("gz", "gx", "gy"), P(), P(), P())
    out_specs = P(None, ("gx", "gz"), "gy")
    return jax.shard_map(body, mesh=mesh, in_specs=in_specs, out_specs=out_specs, check_vma=False)
```

```python
import functools
import math

import jax
import jax.numpy as jnp
from jax import lax
from jax.experimental import pallas as pl
from jax.experimental.pallas import tpu as pltpu
from jax.sharding import PartitionSpec as P

extinction = 1.5
LANES = 128
PAD = 8
HALO = 2
STEP = 16
UNROLL = 32
GROUP = 64
AHEAD = 4
SLOTS = 8
QUAD = 4
WEIGHT_MIB = 24
SHADE_MIB = 24
FUSED_MIB = 48
LOG2E = math.log2(math.e)
MIB = 1 << 20
F32 = jnp.float32
BF16 = jnp.bfloat16


def exchanged(first, last, axis):
    count = lax.axis_size(axis)
    forward = [(i, (i + 1) % count) for i in range(count)]
    backward = [(target, source) for source, target in forward]
    return lax.ppermute(last, axis, forward), lax.ppermute(first, axis, backward)


def exchanged_both(both, axis):
    count = lax.axis_size(axis)
    width = both.shape[0] // 2
    if count == 2:
        return lax.ppermute(both, axis, [(0, 1), (1, 0)]), width, 0
    return jnp.concatenate(exchanged(both[:width], both[width:], axis), axis=0), 0, width


def rows_of(shift, count, part):
    return pl.multiple_of(lax.rem(lax.axis_index("gz") + shift, count) * part, 8)


def weigh(peaks, scale, f, optical, before):
    bump = None
    for k in range(peaks.shape[0]):
        gap = f - peaks[k]
        term = jnp.exp2(gap * (gap * (-2.0 * LOG2E)))
        bump = term if bump is None else bump + term
    optical = optical + bump * scale
    after = jnp.exp2(optical)
    return optical, after, before - after


def pack_kernel(field, low, high, x_first, x_last, z_both, cells, totals, sems):
    depth, rows, _ = field.shape
    chunks = depth // STEP

    def fetch(chunk):
        into = cells.at[pl.ds(HALO + chunk * STEP, STEP), pl.ds(PAD, rows), :]
        return pltpu.make_async_copy(field.at[pl.ds(chunk * STEP, STEP)], into, sems.at[chunk])

    for chunk in range(chunks):
        fetch(chunk).start()
    lane = lax.broadcasted_iota(jnp.int32, (rows, LANES), 1)

    def one(block, none):
        offset = 2 + 2 * lax.rem(block, 2)
        group = (lane + (LANES + 2 - offset)) % LANES // 4
        total = jnp.zeros((rows, LANES), F32)
        for half in range(32 // STEP):
            chunk = block * (32 // STEP) + half
            fetch(chunk).wait()
            for step in range(STEP):
                z = chunk * STEP + step
                index = half * STEP + step
                total = jnp.where(group == index, pltpu.roll(cells[HALO + z, pl.ds(PAD, rows), :], 4 * index + offset, 1), total)
                x_first[pl.ds(HALO * z, HALO), :] = cells[HALO + z, pl.ds(PAD, HALO), :]
                x_last[pl.ds(HALO * z, HALO), :] = cells[HALO + z, pl.ds(PAD + rows - HALO, HALO), :]
        totals[block] = total
        return none

    lax.fori_loop(0, depth // 32, one, 0)
    for face in (x_first, x_last):
        face[pl.ds(HALO * depth, PAD), :] = jnp.zeros((PAD, LANES), F32)
    z_both[pl.ds(0, HALO)] = cells[pl.ds(HALO, HALO), pl.ds(PAD, rows), :]
    z_both[pl.ds(HALO, HALO)] = cells[pl.ds(depth, HALO), pl.ds(PAD, rows), :]
    odd = lane % 4 >= 2
    for block in range(depth // 64):
        one_half, two_half = totals[2 * block], totals[2 * block + 1]
        low[block] = jnp.where(odd, one_half, two_half)
        high[block] = jnp.where(odd, two_half, one_half)


def weight_kernel(scale, shift, count, part, peaks, cells, weight, through, optical):
    depth = weight.shape[0]
    at = pl.ds(pl.multiple_of(rows_of(shift, count, part) + PAD, 8), part)
    optical[...] = jnp.zeros_like(optical)
    through[...] = jnp.ones_like(through)

    def one(turn, none):
        depths, passed = optical[...], through[...]
        for step in range(UNROLL):
            z = turn * UNROLL + step
            depths, passed, weight[z] = weigh(peaks, scale, cells[HALO + z, at, :], depths, passed)
        optical[...], through[...] = depths, passed
        return none

    lax.fori_loop(0, depth // UNROLL, one, 0)


def split(f):
    upper = f.astype(BF16)
    return upper, (f - upper.astype(F32)).astype(BF16)


def edges(begin, part, low_halo, high_halo, low, high, edge):
    at = pl.ds(begin, part)
    place = lax.broadcasted_iota(jnp.int32, (part, LANES), 1) % 4
    for block in range(low.shape[0]):
        below = low_halo[block, at, :] - high[block, at, :]
        above = high_halo[block, at, :] - low[block, at, :]
        for half in range(2):
            if half == 1:
                below, above = pltpu.roll(below, LANES - 2, 1), pltpu.roll(above, LANES - 2, 1)
            right = jnp.where(place == 1, pltpu.roll(above, LANES - 1, 1), 0.0) - 0.125 * pltpu.roll(above, LANES - 2, 1)
            left = 0.125 * pltpu.roll(below, 2, 1) - jnp.where(place == 2, pltpu.roll(below, 1, 1), 0.0)
            edge[2 * block + half] = jnp.where(place < 2, right, left)


def slope_of(ahead):
    near = jnp.where(ahead == 1, 1.0, jnp.where(ahead == -1, -1.0, 0.0))
    return near + jnp.where(ahead == 2, -0.125, jnp.where(ahead == -2, 0.125, 0.0))


def lane_matrix():
    row = lax.broadcasted_iota(jnp.int32, (2 * LANES, LANES), 0)
    column = lax.broadcasted_iota(jnp.int32, (2 * LANES, LANES), 1)
    return slope_of((row - column + 2 * LANES + LANES // 2) % LANES - LANES // 2).astype(BF16)


def row_matrix(group):
    width = group + 2 * PAD
    row = lax.broadcasted_iota(jnp.int32, (group, width), 0)
    column = lax.broadcasted_iota(jnp.int32, (group, width), 1)
    cell = jnp.where(column < group, column, jnp.where(column < group + PAD, column - group - PAD, column - PAD))
    slope = slope_of(cell - row)
    return jnp.concatenate([slope, slope], axis=1).astype(BF16)


def shade_kernel(shift, count, part, group, lower_at, upper_at, scale, peaks, tint, light, *refs):
    cells, weight, through, *refs = refs
    x_low, x_high, z_both, low_halo, high_halo, low, high, out, edge, lanes, across, slopes, strips = refs
    depth, rows = cells.shape[0] - 2 * HALO, low.shape[1]
    turns = depth // UNROLL
    begin = rows_of(shift, count, part)
    lowest, highest = begin == 0, begin + part == rows

    def beside(turn, none):
        for step in range(UNROLL):
            plane = cells.at[HALO + turn * UNROLL + step]
            below, above = plane[pl.ds(begin, PAD), :], plane[pl.ds(pl.multiple_of(begin + PAD + part, 8), PAD), :]
            strips[turn * UNROLL + step, pl.ds(0, PAD), :] = jnp.where(lowest, 0.0, below)
            strips[turn * UNROLL + step, pl.ds(PAD, PAD), :] = jnp.where(highest, 0.0, above)
        return none

    def beside_halo(turn, none, row, halo):
        for step in range(UNROLL):
            z = turn * UNROLL + step
            strips[z, pl.ds(row, HALO), :] = halo[pl.ds(HALO * z, HALO), :]
        return none

    lax.fori_loop(0, turns, beside, 0)

    @pl.when(lowest)
    def _():
        lax.fori_loop(0, turns, functools.partial(beside_halo, row=PAD - HALO, halo=x_low), 0)

    @pl.when(highest)
    def _():
        lax.fori_loop(0, turns, functools.partial(beside_halo, row=PAD, halo=x_high), 0)

    lanes[...] = lane_matrix()
    across[...] = row_matrix(group)
    edges(begin, part, low_halo, high_halo, low, high, edge)
    lane = lax.broadcasted_iota(jnp.int32, (group, LANES), 1)
    rim = (lane < HALO) | (lane >= LANES - HALO)
    for start in range(0, part, group):
        row = pl.multiple_of(begin + start, 8)

        def halved(first, number):
            inner, outer = [], []
            for step in range(number):
                plane = cells.at[HALO + first + step]
                inner.append(split(plane[pl.ds(pl.multiple_of(row + PAD, 8), group), :]))
                below = strips[first + step, pl.ds(0, PAD), :] if start == 0 else plane[pl.ds(row, PAD), :]
                if start + group == part:
                    above = strips[first + step, pl.ds(PAD, PAD), :]
                else:
                    above = plane[pl.ds(pl.multiple_of(row + PAD + group, 8), PAD), :]
                outer.append(split(jnp.concatenate([below, above], axis=0)))
            return inner, outer

        def prepare(first, place):
            kept = edge[first // 32, pl.ds(start, group), :]
            halves, sides = halved(first, QUAD)
            rows_in = jnp.concatenate([jnp.concatenate(half, axis=1) for half in halves], axis=0)
            along_y = jnp.dot(rows_in, lanes[...], preferred_element_type=F32)[:, :LANES]
            for step in range(QUAD):
                turn = lax.rem(2 * LANES - 2 - 4 * lax.rem(first + step, 32), LANES)
                fix = jnp.where(rim, pltpu.roll(kept, turn, 1), 0.0)
                slopes[(place + step) % SLOTS, 1] = along_y[step * group : (step + 1) * group] + fix
            for pair in range(0, QUAD, 2):
                both = [
                    jnp.concatenate([rows[pair][k], rows[pair + 1][k]], axis=1) for k in range(2) for rows in (halves, sides)
                ]
                along_x = jnp.dot(across[...], jnp.concatenate(both, axis=0), preferred_element_type=F32)
                for step in range(2):
                    slopes[(place + pair + step) % SLOTS, 0] = along_x[:, step * LANES : (step + 1) * LANES]

        def use(turn, step, carry):
            z, place = turn * UNROLL + step, step
            sums = carry

            def at(dz):
                layer = cells[HALO + z + dz, pl.ds(pl.multiple_of(row + PAD, 8), group), :]
                if step + dz < 0:
                    layer = jnp.where(turn == 0, z_both[lower_at + HALO + step + dz, pl.ds(row, group), :], layer)
                if step + dz >= UNROLL:
                    beyond = z_both[upper_at + step + dz - UNROLL, pl.ds(row, group), :]
                    layer = jnp.where(turn == turns - 1, beyond, layer)
                return layer

            f = at(0)
            qx, qy = slopes[place % SLOTS, 0], slopes[place % SLOTS, 1]
            qz = (at(1) - at(-1)) - 0.125 * (at(2) - at(-2))
            along = qx * (0.7 * light[0]) + qy * (0.7 * light[1]) + qz * (0.7 * light[2])
            inverse = lax.rsqrt(qx * qx + qy * qy + qz * qz + 2.25)
            own = weight[z, pl.ds(start, group), :]
            lit = own * (0.3 + jnp.abs(along * inverse))
            return (sums[0] + lit,) + tuple(sums[c + 1] + lit * jnp.tanh(f * (0.5 * tint[c])) for c in range(3))

        def one(turn, carry):
            for step in range(0, UNROLL, QUAD):
                z = turn * UNROLL + step
                later = z + AHEAD
                if step + AHEAD >= UNROLL:
                    later = jnp.minimum(later, depth - QUAD)
                prepare(later, step + AHEAD)
                for near in range(QUAD):
                    carry = use(turn, step + near, carry)
            return carry

        for step in range(0, AHEAD, QUAD):
            prepare(step, step)
        zero = jnp.zeros((group, LANES), F32)
        carry = lax.fori_loop(0, turns, one, (zero,) * 4)
        for c in range(3):
            out[c, pl.ds(start, group), :] = 0.5 * (carry[0] + carry[c + 1])
        out[3, pl.ds(start, group), :] = through[pl.ds(start, group), :]


def fetches(shift, count, part, field, cells, sems):
    _, rows, _ = field.shape
    begin = rows_of(shift, count, part)
    below = pl.multiple_of(jnp.maximum(begin - PAD, 0), 8)
    above = pl.multiple_of(jnp.minimum(begin + part, rows - PAD), 8)

    def fetch(chunk):
        at = pl.ds(chunk * STEP, STEP)
        into = pl.ds(HALO + chunk * STEP, STEP)
        return (
            pltpu.make_async_copy(field.at[at, pl.ds(begin, part), :], cells.at[into, pl.ds(PAD, part), :], sems.at[0, chunk]),
            pltpu.make_async_copy(field.at[at, pl.ds(below, PAD), :], cells.at[into, pl.ds(0, PAD), :], sems.at[1, chunk]),
            pltpu.make_async_copy(field.at[at, pl.ds(above, PAD), :], cells.at[into, pl.ds(PAD + part, PAD), :], sems.at[2, chunk]),
        )

    return fetch


def fused_kernel(shift, count, part, group, lower_at, upper_at, scale, peaks, tint, light, *refs):
    field, *refs = refs
    x_low, x_high, z_both, low_halo, high_halo, low, high, out, cells, edge, lanes, across, slopes, sems = refs
    depth = field.shape[0]
    fetch = fetches(shift, count, part, field, cells, sems)
    rows = z_both.shape[1]
    chunks = depth // STEP
    turns = depth // UNROLL
    begin = rows_of(shift, count, part)
    main = pl.ds(PAD, part)

    for chunk in range(chunks):
        for copy in fetch(chunk):
            copy.start()
    lanes[...] = lane_matrix()
    across[...] = row_matrix(group)
    edges(begin, part, low_halo, high_halo, low, high, edge)
    cells[pl.ds(0, HALO), main, :] = z_both[pl.ds(lower_at, HALO), pl.ds(begin, part), :]
    cells[pl.ds(HALO + depth, HALO), main, :] = z_both[pl.ds(upper_at, HALO), pl.ds(begin, part), :]

    def beside(first, number):
        @pl.when(begin == 0)
        def _():
            for step in range(number):
                cells[HALO + first + step, pl.ds(PAD - HALO, HALO), :] = x_low[pl.ds(HALO * (first + step), HALO), :]

        @pl.when(begin + part == rows)
        def _():
            for step in range(number):
                cells[HALO + first + step, pl.ds(PAD + part, HALO), :] = x_high[pl.ds(HALO * (first + step), HALO), :]

    def arrive(chunk, number):
        for ahead in range(number):
            for copy in fetch(chunk + ahead):
                copy.wait()
        beside(chunk * STEP, number * STEP)

    arrive(0, 1)
    lane = lax.broadcasted_iota(jnp.int32, (group, LANES), 1)
    rim = (lane < HALO) | (lane >= LANES - HALO)
    for start in range(0, part, group):

        def halved(first, number):
            inner, outer = [], []
            for step in range(number):
                plane = cells.at[HALO + first + step]
                inner.append(split(plane[pl.ds(PAD + start, group), :]))
                below, above = plane[pl.ds(start, PAD), :], plane[pl.ds(PAD + start + group, PAD), :]
                outer.append(split(jnp.concatenate([below, above], axis=0)))
            return inner, outer

        def prepare(first, place):
            kept = edge[first // 32, pl.ds(start, group), :]
            halves, sides = halved(first, QUAD)
            rows_in = jnp.concatenate([jnp.concatenate(half, axis=1) for half in halves], axis=0)
            along_y = jnp.dot(rows_in, lanes[...], preferred_element_type=F32)[:, :LANES]
            for step in range(QUAD):
                turn = lax.rem(2 * LANES - 2 - 4 * lax.rem(first + step, 32), LANES)
                fix = jnp.where(rim, pltpu.roll(kept, turn, 1), 0.0)
                slopes[(place + step) % SLOTS, 1] = along_y[step * group : (step + 1) * group] + fix
            for pair in range(0, QUAD, 2):
                both = [
                    jnp.concatenate([rows[pair][k], rows[pair + 1][k]], axis=1) for k in range(2) for rows in (halves, sides)
                ]
                along_x = jnp.dot(across[...], jnp.concatenate(both, axis=0), preferred_element_type=F32)
                for step in range(2):
                    slopes[(place + pair + step) % SLOTS, 0] = along_x[:, step * LANES : (step + 1) * LANES]

        def use(z, place, carry):
            sums, seen = carry[:4], carry[4:]

            def at(dz):
                return cells[HALO + z + dz, pl.ds(PAD + start, group), :]

            f = at(0)
            qx, qy = slopes[place % SLOTS, 0], slopes[place % SLOTS, 1]
            qz = (at(1) - at(-1)) - 0.125 * (at(2) - at(-2))
            along = qx * (0.7 * light[0]) + qy * (0.7 * light[1]) + qz * (0.7 * light[2])
            inverse = lax.rsqrt(qx * qx + qy * qy + qz * qz + 2.25)
            optical, passed, own = weigh(peaks, scale, f, *seen)
            seen = (optical, passed)
            lit = own * (0.3 + jnp.abs(along * inverse))
            return (sums[0] + lit,) + tuple(sums[c + 1] + lit * jnp.tanh(f * (0.5 * tint[c])) for c in range(3)) + seen

        def one(turn, carry):
            if start == 0:
                chunk = turn * (UNROLL // STEP) + 1

                @pl.when(turn + 1 < turns)
                def _():
                    arrive(chunk, UNROLL // STEP)

                @pl.when(turn + 1 == turns)
                def _():
                    arrive(chunk, UNROLL // STEP - 1)

            for step in range(0, UNROLL, QUAD):
                z = turn * UNROLL + step
                later = z + AHEAD
                if step + AHEAD >= UNROLL:
                    later = jnp.minimum(later, depth - QUAD)
                prepare(later, step + AHEAD)
                for near in range(QUAD):
                    carry = use(z + near, step + near, carry)
            return carry

        for step in range(0, AHEAD, QUAD):
            prepare(step, step)
        zero = jnp.zeros((group, LANES), F32)
        carry = lax.fori_loop(0, turns, one, (zero,) * 5 + (zero + 1.0,))
        for c in range(3):
            out[c, pl.ds(start, group), :] = 0.5 * (carry[0] + carry[c + 1])
        out[3, pl.ds(start, group), :] = carry[5]


SMEM = pl.BlockSpec(memory_space=pltpu.SMEM)
VMEM = pl.BlockSpec(memory_space=pltpu.VMEM)
HBM = pl.BlockSpec(memory_space=pltpu.HBM)


def cost(cells, flops, terms):
    return pl.CostEstimate(flops=cells * flops, bytes_accessed=cells * 8, transcendentals=cells * terms)


def body(field, peaks, tint, light):
    depth, rows, lanes = field.shape
    count = lax.axis_size("gz")
    part = rows // count
    cells = depth * rows * lanes
    chunks = depth // STEP
    shape = jax.ShapeDtypeStruct
    scale = -extinction / (depth * count) * LOG2E

    def params(mib):
        return pltpu.CompilerParams(vmem_limit_bytes=mib * MIB)

    padded = (depth + 2 * HALO, rows + 2 * PAD, lanes)
    low, high, x_first, x_last, z_own, cells_in = pl.pallas_call(
        pack_kernel,
        out_shape=(
            pltpu.VMEM((depth // 64, rows, lanes), F32),
            pltpu.VMEM((depth // 64, rows, lanes), F32),
            pltpu.VMEM((HALO * depth + PAD, lanes), F32),
            pltpu.VMEM((HALO * depth + PAD, lanes), F32),
            pltpu.VMEM((2 * HALO, rows, lanes), F32),
            pltpu.VMEM(padded, F32),
        ),
        in_specs=[HBM],
        out_specs=(VMEM,) * 6,
        scratch_shapes=[
            pltpu.VMEM((depth // 32, rows, lanes), F32),
            pltpu.SemaphoreType.DMA((chunks,)),
        ],
        compiler_params=params(48),
        cost_estimate=cost(cells, 10, 0),
        name="pack",
    )(field)
    x_low, x_high = exchanged(x_first, x_last, "gx")
    z_both, lower_at, upper_at = exchanged_both(z_own, "gz")
    low_halo, high_halo = exchanged(low, high, "gy")

    group = min(GROUP, part)
    weight, through = pl.pallas_call(
        functools.partial(weight_kernel, scale, 1, count, part),
        out_shape=(pltpu.VMEM((depth, part, lanes), F32), shape((part, lanes), F32)),
        in_specs=[SMEM, VMEM],
        out_specs=(VMEM, VMEM),
        scratch_shapes=[pltpu.VMEM((part, lanes), F32)],
        compiler_params=params(WEIGHT_MIB),
        cost_estimate=cost(cells // count, 18, 5),
        name="weights",
    )(peaks, cells_in)

    pieces = []
    for turn in range(count):
        shift = (turn + 1) % count
        ready = turn == 0
        operands = [peaks, tint, light] + ([cells_in, weight, through] if ready else [field])
        halos = [x_low, x_high, z_both, low_halo, high_halo, low, high]
        scratch = [
            pltpu.VMEM((depth // 32, part, lanes), F32),
            pltpu.VMEM((2 * lanes, lanes), BF16),
            pltpu.VMEM((group, 2 * (group + 2 * PAD)), BF16),
            pltpu.VMEM((SLOTS, 2, group, lanes), F32),
        ]
        if ready:
            scratch.append(pltpu.VMEM((depth, 2 * PAD, lanes), F32))
        else:
            own_cells = pltpu.VMEM((depth + 2 * HALO, part + 2 * PAD, lanes), F32)
            scratch = [own_cells] + scratch + [pltpu.SemaphoreType.DMA((3, chunks))]
        result = shape((4, part, lanes), F32)
        piece = pl.pallas_call(
            functools.partial(shade_kernel if ready else fused_kernel, shift, count, part, group, lower_at, upper_at, scale),
            out_shape=result,
            in_specs=[SMEM] * 3 + ([VMEM] * 3 if ready else [HBM]) + [VMEM] * len(halos),
            out_specs=VMEM,
            scratch_shapes=scratch,
            compiler_params=params(SHADE_MIB if ready else FUSED_MIB),
            cost_estimate=cost(cells // count, 40, 4),
            name="shade" if ready else "fused",
        )(*operands, *halos)
        if shift:
            piece = lax.ppermute(piece, "gz", [(i, (i + shift) % count) for i in range(count)])
        pieces.append((lax.rem(lax.axis_index("gz") + count - shift, count), piece))

    image = 0.0
    for source, piece in pieces:
        for other, rest in pieces:
            if other is not source:
                piece = piece * jnp.where(other < source, rest[3:], 1.0)
        image = image + piece
    total = functools.reduce(jnp.multiply, [piece[3:] for _, piece in pieces])
    channel = lax.broadcasted_iota(jnp.int32, image.shape, 0)
    return jnp.where(channel < 3, image, 1.0 - total)


def solution(mesh):
    in_specs = (P("gz", "gx", "gy"), P(), P(), P())
    out_specs = P(None, ("gx", "gz"), "gy")
    return jax.shard_map(body, mesh=mesh, in_specs=in_specs, out_specs=out_specs, check_vma=False)
```

```python
import functools
import math

import jax
import jax.numpy as jnp
from jax import lax
from jax.experimental import pallas as pl
from jax.experimental.pallas import tpu as pltpu
from jax.sharding import PartitionSpec as P

extinction = 1.5
LANES = 128
PAD = 8
HALO = 2
STEP = 16
UNROLL = 32
GROUP = 64
AHEAD = 4
SLOTS = 8
QUAD = 4
WEIGHT_MIB = 24
SHADE_MIB = 24
FUSED_MIB = 48
LOG2E = math.log2(math.e)
MIB = 1 << 20
F32 = jnp.float32
BF16 = jnp.bfloat16


def exchanged(first, last, axis):
    count = lax.axis_size(axis)
    forward = [(i, (i + 1) % count) for i in range(count)]
    backward = [(target, source) for source, target in forward]
    return lax.ppermute(last, axis, forward), lax.ppermute(first, axis, backward)


def exchanged_both(both, axis):
    count = lax.axis_size(axis)
    width = both.shape[0] // 2
    if count == 2:
        return lax.ppermute(both, axis, [(0, 1), (1, 0)]), width, 0
    return jnp.concatenate(exchanged(both[:width], both[width:], axis), axis=0), 0, width


def rows_of(shift, count, part):
    return pl.multiple_of(lax.rem(lax.axis_index("gz") + shift, count) * part, 8)


def weigh(peaks, scale, f, optical, before):
    bump = None
    for k in range(peaks.shape[0]):
        gap = f - peaks[k]
        term = jnp.exp2(gap * (gap * (-2.0 * LOG2E)))
        bump = term if bump is None else bump + term
    optical = optical + bump * scale
    after = jnp.exp2(optical)
    return optical, after, before - after


def pack_kernel(field, low, high, x_first, x_last, z_both, cells, totals, sems):
    depth, rows, _ = field.shape
    chunks = depth // STEP

    def fetch(chunk):
        into = cells.at[pl.ds(HALO + chunk * STEP, STEP), pl.ds(PAD, rows), :]
        return pltpu.make_async_copy(field.at[pl.ds(chunk * STEP, STEP)], into, sems.at[chunk])

    for chunk in range(chunks):
        fetch(chunk).start()
    lane = lax.broadcasted_iota(jnp.int32, (rows, LANES), 1)

    def one(block, none):
        offset = 2 + 2 * lax.rem(block, 2)
        group = (lane + (LANES + 2 - offset)) % LANES // 4
        total = jnp.zeros((rows, LANES), F32)
        for half in range(32 // STEP):
            chunk = block * (32 // STEP) + half
            fetch(chunk).wait()
            for step in range(STEP):
                z = chunk * STEP + step
                index = half * STEP + step
                total = jnp.where(group == index, pltpu.roll(cells[HALO + z, pl.ds(PAD, rows), :], 4 * index + offset, 1), total)
                x_first[pl.ds(HALO * z, HALO), :] = cells[HALO + z, pl.ds(PAD, HALO), :]
                x_last[pl.ds(HALO * z, HALO), :] = cells[HALO + z, pl.ds(PAD + rows - HALO, HALO), :]
        totals[block] = total
        return none

    lax.fori_loop(0, depth // 32, one, 0)
    for face in (x_first, x_last):
        face[pl.ds(HALO * depth, PAD), :] = jnp.zeros((PAD, LANES), F32)
    z_both[pl.ds(0, HALO)] = cells[pl.ds(HALO, HALO), pl.ds(PAD, rows), :]
    z_both[pl.ds(HALO, HALO)] = cells[pl.ds(depth, HALO), pl.ds(PAD, rows), :]
    odd = lane % 4 >= 2
    for block in range(depth // 64):
        one_half, two_half = totals[2 * block], totals[2 * block + 1]
        low[block] = jnp.where(odd, one_half, two_half)
        high[block] = jnp.where(odd, two_half, one_half)


def weight_kernel(scale, shift, count, part, peaks, cells, weight, through, optical):
    depth = weight.shape[0]
    at = pl.ds(pl.multiple_of(rows_of(shift, count, part) + PAD, 8), part)
    optical[...] = jnp.zeros_like(optical)
    through[...] = jnp.ones_like(through)

    def one(turn, none):
        depths, passed = optical[...], through[...]
        for step in range(UNROLL):
            z = turn * UNROLL + step
            depths, passed, weight[z] = weigh(peaks, scale, cells[HALO + z, at, :], depths, passed)
        optical[...], through[...] = depths, passed
        return none

    lax.fori_loop(0, depth // UNROLL, one, 0)


def split(f):
    upper = f.astype(BF16)
    return upper, (f - upper.astype(F32)).astype(BF16)


def edges(begin, part, low_halo, high_halo, low, high, edge):
    at = pl.ds(begin, part)
    place = lax.broadcasted_iota(jnp.int32, (part, LANES), 1) % 4
    for block in range(low.shape[0]):
        below = low_halo[block, at, :] - high[block, at, :]
        above = high_halo[block, at, :] - low[block, at, :]
        for half in range(2):
            if half == 1:
                below, above = pltpu.roll(below, LANES - 2, 1), pltpu.roll(above, LANES - 2, 1)
            right = jnp.where(place == 1, pltpu.roll(above, LANES - 1, 1), 0.0) - 0.125 * pltpu.roll(above, LANES - 2, 1)
            left = 0.125 * pltpu.roll(below, 2, 1) - jnp.where(place == 2, pltpu.roll(below, 1, 1), 0.0)
            edge[2 * block + half] = jnp.where(place < 2, right, left)


def slope_of(ahead):
    near = jnp.where(ahead == 1, 1.0, jnp.where(ahead == -1, -1.0, 0.0))
    return near + jnp.where(ahead == 2, -0.125, jnp.where(ahead == -2, 0.125, 0.0))


def lane_matrix():
    row = lax.broadcasted_iota(jnp.int32, (2 * LANES, LANES), 0)
    column = lax.broadcasted_iota(jnp.int32, (2 * LANES, LANES), 1)
    return slope_of((row - column + 2 * LANES + LANES // 2) % LANES - LANES // 2).astype(BF16)


def row_matrix(group):
    width = group + 2 * PAD
    row = lax.broadcasted_iota(jnp.int32, (group, width), 0)
    column = lax.broadcasted_iota(jnp.int32, (group, width), 1)
    cell = jnp.where(column < group, column, jnp.where(column < group + PAD, column - group - PAD, column - PAD))
    slope = slope_of(cell - row)
    return jnp.concatenate([slope, slope], axis=1).astype(BF16)


def shade_kernel(shift, count, part, group, lower_at, upper_at, scale, peaks, tint, light, *refs):
    cells, weight, through, *refs = refs
    x_low, x_high, z_both, low_halo, high_halo, low, high, out, edge, lanes, across, slopes, strips = refs
    depth, rows = cells.shape[0] - 2 * HALO, low.shape[1]
    turns = depth // UNROLL
    begin = rows_of(shift, count, part)
    lowest, highest = begin == 0, begin + part == rows

    def beside(turn, none):
        for step in range(UNROLL):
            plane = cells.at[HALO + turn * UNROLL + step]
            below, above = plane[pl.ds(begin, PAD), :], plane[pl.ds(pl.multiple_of(begin + PAD + part, 8), PAD), :]
            strips[turn * UNROLL + step, pl.ds(0, PAD), :] = jnp.where(lowest, 0.0, below)
            strips[turn * UNROLL + step, pl.ds(PAD, PAD), :] = jnp.where(highest, 0.0, above)
        return none

    def beside_halo(turn, none, row, halo):
        for step in range(UNROLL):
            z = turn * UNROLL + step
            strips[z, pl.ds(row, HALO), :] = halo[pl.ds(HALO * z, HALO), :]
        return none

    lax.fori_loop(0, turns, beside, 0)

    @pl.when(lowest)
    def _():
        lax.fori_loop(0, turns, functools.partial(beside_halo, row=PAD - HALO, halo=x_low), 0)

    @pl.when(highest)
    def _():
        lax.fori_loop(0, turns, functools.partial(beside_halo, row=PAD, halo=x_high), 0)

    lanes[...] = lane_matrix()
    across[...] = row_matrix(group)
    edges(begin, part, low_halo, high_halo, low, high, edge)
    lane = lax.broadcasted_iota(jnp.int32, (group, LANES), 1)
    rim = (lane < HALO) | (lane >= LANES - HALO)
    for start in range(0, part, group):
        row = pl.multiple_of(begin + start, 8)

        def halved(first, number):
            inner, outer = [], []
            for step in range(number):
                plane = cells.at[HALO + first + step]
                inner.append(split(plane[pl.ds(pl.multiple_of(row + PAD, 8), group), :]))
                below = strips[first + step, pl.ds(0, PAD), :] if start == 0 else plane[pl.ds(row, PAD), :]
                if start + group == part:
                    above = strips[first + step, pl.ds(PAD, PAD), :]
                else:
                    above = plane[pl.ds(pl.multiple_of(row + PAD + group, 8), PAD), :]
                outer.append(split(jnp.concatenate([below, above], axis=0)))
            return inner, outer

        def prepare(first, place):
            kept = edge[first // 32, pl.ds(start, group), :]
            halves, sides = halved(first, QUAD)
            rows_in = jnp.concatenate([jnp.concatenate(half, axis=1) for half in halves], axis=0)
            along_y = jnp.dot(rows_in, lanes[...], preferred_element_type=F32)[:, :LANES]
            for step in range(QUAD):
                turn = lax.rem(2 * LANES - 2 - 4 * lax.rem(first + step, 32), LANES)
                fix = jnp.where(rim, pltpu.roll(kept, turn, 1), 0.0)
                slopes[(place + step) % SLOTS, 1] = along_y[step * group : (step + 1) * group] + fix
            for pair in range(0, QUAD, 2):
                both = [
                    jnp.concatenate([rows[pair][k], rows[pair + 1][k]], axis=1) for k in range(2) for rows in (halves, sides)
                ]
                along_x = jnp.dot(across[...], jnp.concatenate(both, axis=0), preferred_element_type=F32)
                for step in range(2):
                    slopes[(place + pair + step) % SLOTS, 0] = along_x[:, step * LANES : (step + 1) * LANES]

        def use(turn, step, carry):
            z, place = turn * UNROLL + step, step
            sums = carry

            def at(dz):
                layer = cells[HALO + z + dz, pl.ds(pl.multiple_of(row + PAD, 8), group), :]
                if step + dz < 0:
                    layer = jnp.where(turn == 0, z_both[lower_at + HALO + step + dz, pl.ds(row, group), :], layer)
                if step + dz >= UNROLL:
                    beyond = z_both[upper_at + step + dz - UNROLL, pl.ds(row, group), :]
                    layer = jnp.where(turn == turns - 1, beyond, layer)
                return layer

            f = at(0)
            qx, qy = slopes[place % SLOTS, 0], slopes[place % SLOTS, 1]
            qz = (at(1) - at(-1)) - 0.125 * (at(2) - at(-2))
            along = qx * (0.7 * light[0]) + qy * (0.7 * light[1]) + qz * (0.7 * light[2])
            inverse = lax.rsqrt(qx * qx + qy * qy + qz * qz + 2.25)
            own = weight[z, pl.ds(start, group), :]
            lit = own * (0.3 + jnp.abs(along * inverse))
            return (sums[0] + lit,) + tuple(sums[c + 1] + lit * jnp.tanh(f * (0.5 * tint[c])) for c in range(3))

        def one(turn, carry):
            for step in range(0, UNROLL, QUAD):
                z = turn * UNROLL + step
                later = z + AHEAD
                if step + AHEAD >= UNROLL:
                    later = jnp.minimum(later, depth - QUAD)
                prepare(later, step + AHEAD)
                for near in range(QUAD):
                    carry = use(turn, step + near, carry)
            return carry

        for step in range(0, AHEAD, QUAD):
            prepare(step, step)
        zero = jnp.zeros((group, LANES), F32)
        carry = lax.fori_loop(0, turns, one, (zero,) * 4)
        for c in range(3):
            out[c, pl.ds(start, group), :] = 0.5 * (carry[0] + carry[c + 1])
        out[3, pl.ds(start, group), :] = through[pl.ds(start, group), :]


def fetches(shift, count, part, field, cells, sems):
    _, rows, _ = field.shape
    begin = rows_of(shift, count, part)
    below = pl.multiple_of(jnp.maximum(begin - PAD, 0), 8)
    above = pl.multiple_of(jnp.minimum(begin + part, rows - PAD), 8)

    def fetch(chunk):
        at = pl.ds(chunk * STEP, STEP)
        into = pl.ds(HALO + chunk * STEP, STEP)
        return (
            pltpu.make_async_copy(field.at[at, pl.ds(begin, part), :], cells.at[into, pl.ds(PAD, part), :], sems.at[0, chunk]),
            pltpu.make_async_copy(field.at[at, pl.ds(below, PAD), :], cells.at[into, pl.ds(0, PAD), :], sems.at[1, chunk]),
            pltpu.make_async_copy(field.at[at, pl.ds(above, PAD), :], cells.at[into, pl.ds(PAD + part, PAD), :], sems.at[2, chunk]),
        )

    return fetch


def fused_kernel(shift, count, part, group, lower_at, upper_at, scale, peaks, tint, light, *refs):
    field, *refs = refs
    x_low, x_high, z_both, low_halo, high_halo, low, high, out, cells, edge, lanes, across, slopes, sems = refs
    depth = field.shape[0]
    fetch = fetches(shift, count, part, field, cells, sems)
    rows = z_both.shape[1]
    chunks = depth // STEP
    turns = depth // UNROLL
    begin = rows_of(shift, count, part)
    main = pl.ds(PAD, part)

    soon = min(UNROLL // STEP + 1, chunks)
    for chunk in range(soon):
        for copy in fetch(chunk):
            copy.start()
    lanes[...] = lane_matrix()
    across[...] = row_matrix(group)
    edges(begin, part, low_halo, high_halo, low, high, edge)
    cells[pl.ds(0, HALO), main, :] = z_both[pl.ds(lower_at, HALO), pl.ds(begin, part), :]
    cells[pl.ds(HALO + depth, HALO), main, :] = z_both[pl.ds(upper_at, HALO), pl.ds(begin, part), :]

    def beside(first, number):
        @pl.when(begin == 0)
        def _():
            for step in range(number):
                cells[HALO + first + step, pl.ds(PAD - HALO, HALO), :] = x_low[pl.ds(HALO * (first + step), HALO), :]

        @pl.when(begin + part == rows)
        def _():
            for step in range(number):
                cells[HALO + first + step, pl.ds(PAD + part, HALO), :] = x_high[pl.ds(HALO * (first + step), HALO), :]

    def arrive(chunk, number):
        for ahead in range(number):
            for copy in fetch(chunk + ahead):
                copy.wait()
        beside(chunk * STEP, number * STEP)

    for chunk in range(soon, chunks):
        for copy in fetch(chunk):
            copy.start()
    arrive(0, 1)
    lane = lax.broadcasted_iota(jnp.int32, (group, LANES), 1)
    rim = (lane < HALO) | (lane >= LANES - HALO)
    for start in range(0, part, group):

        def halved(first, number):
            inner, outer = [], []
            for step in range(number):
                plane = cells.at[HALO + first + step]
                inner.append(split(plane[pl.ds(PAD + start, group), :]))
                below, above = plane[pl.ds(start, PAD), :], plane[pl.ds(PAD + start + group, PAD), :]
                outer.append(split(jnp.concatenate([below, above], axis=0)))
            return inner, outer

        def prepare(first, place):
            kept = edge[first // 32, pl.ds(start, group), :]
            halves, sides = halved(first, QUAD)
            rows_in = jnp.concatenate([jnp.concatenate(half, axis=1) for half in halves], axis=0)
            along_y = jnp.dot(rows_in, lanes[...], preferred_element_type=F32)[:, :LANES]
            for step in range(QUAD):
                turn = lax.rem(2 * LANES - 2 - 4 * lax.rem(first + step, 32), LANES)
                fix = jnp.where(rim, pltpu.roll(kept, turn, 1), 0.0)
                slopes[(place + step) % SLOTS, 1] = along_y[step * group : (step + 1) * group] + fix
            for pair in range(0, QUAD, 2):
                both = [
                    jnp.concatenate([rows[pair][k], rows[pair + 1][k]], axis=1) for k in range(2) for rows in (halves, sides)
                ]
                along_x = jnp.dot(across[...], jnp.concatenate(both, axis=0), preferred_element_type=F32)
                for step in range(2):
                    slopes[(place + pair + step) % SLOTS, 0] = along_x[:, step * LANES : (step + 1) * LANES]

        def use(z, place, carry):
            sums, seen = carry[:4], carry[4:]

            def at(dz):
                return cells[HALO + z + dz, pl.ds(PAD + start, group), :]

            f = at(0)
            qx, qy = slopes[place % SLOTS, 0], slopes[place % SLOTS, 1]
            qz = (at(1) - at(-1)) - 0.125 * (at(2) - at(-2))
            along = qx * (0.7 * light[0]) + qy * (0.7 * light[1]) + qz * (0.7 * light[2])
            inverse = lax.rsqrt(qx * qx + qy * qy + qz * qz + 2.25)
            optical, passed, own = weigh(peaks, scale, f, *seen)
            seen = (optical, passed)
            lit = own * (0.3 + jnp.abs(along * inverse))
            return (sums[0] + lit,) + tuple(sums[c + 1] + lit * jnp.tanh(f * (0.5 * tint[c])) for c in range(3)) + seen

        def one(turn, carry):
            if start == 0:
                chunk = turn * (UNROLL // STEP) + 1

                @pl.when(turn + 1 < turns)
                def _():
                    arrive(chunk, UNROLL // STEP)

                @pl.when(turn + 1 == turns)
                def _():
                    arrive(chunk, UNROLL // STEP - 1)

            for step in range(0, UNROLL, QUAD):
                z = turn * UNROLL + step
                later = z + AHEAD
                if step + AHEAD >= UNROLL:
                    later = jnp.minimum(later, depth - QUAD)
                prepare(later, step + AHEAD)
                for near in range(QUAD):
                    carry = use(z + near, step + near, carry)
            return carry

        for step in range(0, AHEAD, QUAD):
            prepare(step, step)
        zero = jnp.zeros((group, LANES), F32)
        carry = lax.fori_loop(0, turns, one, (zero,) * 5 + (zero + 1.0,))
        for c in range(3):
            out[c, pl.ds(start, group), :] = 0.5 * (carry[0] + carry[c + 1])
        out[3, pl.ds(start, group), :] = carry[5]


SMEM = pl.BlockSpec(memory_space=pltpu.SMEM)
VMEM = pl.BlockSpec(memory_space=pltpu.VMEM)
HBM = pl.BlockSpec(memory_space=pltpu.HBM)


def cost(cells, flops, terms):
    return pl.CostEstimate(flops=cells * flops, bytes_accessed=cells * 8, transcendentals=cells * terms)


def body(field, peaks, tint, light):
    depth, rows, lanes = field.shape
    count = lax.axis_size("gz")
    part = rows // count
    cells = depth * rows * lanes
    chunks = depth // STEP
    shape = jax.ShapeDtypeStruct
    scale = -extinction / (depth * count) * LOG2E

    def params(mib):
        return pltpu.CompilerParams(vmem_limit_bytes=mib * MIB)

    padded = (depth + 2 * HALO, rows + 2 * PAD, lanes)
    low, high, x_first, x_last, z_own, cells_in = pl.pallas_call(
        pack_kernel,
        out_shape=(
            pltpu.VMEM((depth // 64, rows, lanes), F32),
            pltpu.VMEM((depth // 64, rows, lanes), F32),
            pltpu.VMEM((HALO * depth + PAD, lanes), F32),
            pltpu.VMEM((HALO * depth + PAD, lanes), F32),
            pltpu.VMEM((2 * HALO, rows, lanes), F32),
            pltpu.VMEM(padded, F32),
        ),
        in_specs=[HBM],
        out_specs=(VMEM,) * 6,
        scratch_shapes=[
            pltpu.VMEM((depth // 32, rows, lanes), F32),
            pltpu.SemaphoreType.DMA((chunks,)),
        ],
        compiler_params=params(48),
        cost_estimate=cost(cells, 10, 0),
        name="pack",
    )(field)
    x_low, x_high = exchanged(x_first, x_last, "gx")
    z_both, lower_at, upper_at = exchanged_both(z_own, "gz")
    low_halo, high_halo = exchanged(low, high, "gy")

    group = min(GROUP, part)
    weight, through = pl.pallas_call(
        functools.partial(weight_kernel, scale, 1, count, part),
        out_shape=(pltpu.VMEM((depth, part, lanes), F32), shape((part, lanes), F32)),
        in_specs=[SMEM, VMEM],
        out_specs=(VMEM, VMEM),
        scratch_shapes=[pltpu.VMEM((part, lanes), F32)],
        compiler_params=params(WEIGHT_MIB),
        cost_estimate=cost(cells // count, 18, 5),
        name="weights",
    )(peaks, cells_in)

    pieces = []
    for turn in range(count):
        shift = (turn + 1) % count
        ready = turn == 0
        operands = [peaks, tint, light] + ([cells_in, weight, through] if ready else [field])
        halos = [x_low, x_high, z_both, low_halo, high_halo, low, high]
        scratch = [
            pltpu.VMEM((depth // 32, part, lanes), F32),
            pltpu.VMEM((2 * lanes, lanes), BF16),
            pltpu.VMEM((group, 2 * (group + 2 * PAD)), BF16),
            pltpu.VMEM((SLOTS, 2, group, lanes), F32),
        ]
        if ready:
            scratch.append(pltpu.VMEM((depth, 2 * PAD, lanes), F32))
        else:
            own_cells = pltpu.VMEM((depth + 2 * HALO, part + 2 * PAD, lanes), F32)
            scratch = [own_cells] + scratch + [pltpu.SemaphoreType.DMA((3, chunks))]
        result = shape((4, part, lanes), F32)
        piece = pl.pallas_call(
            functools.partial(shade_kernel if ready else fused_kernel, shift, count, part, group, lower_at, upper_at, scale),
            out_shape=result,
            in_specs=[SMEM] * 3 + ([VMEM] * 3 if ready else [HBM]) + [VMEM] * len(halos),
            out_specs=VMEM,
            scratch_shapes=scratch,
            compiler_params=params(SHADE_MIB if ready else FUSED_MIB),
            cost_estimate=cost(cells // count, 40, 4),
            name="shade" if ready else "fused",
        )(*operands, *halos)
        if shift:
            piece = lax.ppermute(piece, "gz", [(i, (i + shift) % count) for i in range(count)])
        pieces.append((lax.rem(lax.axis_index("gz") + count - shift, count), piece))

    image = 0.0
    for source, piece in pieces:
        for other, rest in pieces:
            if other is not source:
                piece = piece * jnp.where(other < source, rest[3:], 1.0)
        image = image + piece
    total = functools.reduce(jnp.multiply, [piece[3:] for _, piece in pieces])
    channel = lax.broadcasted_iota(jnp.int32, image.shape, 0)
    return jnp.where(channel < 3, image, 1.0 - total)


def solution(mesh):
    in_specs = (P("gz", "gx", "gy"), P(), P(), P())
    out_specs = P(None, ("gx", "gz"), "gy")
    return jax.shard_map(body, mesh=mesh, in_specs=in_specs, out_specs=out_specs, check_vma=False)
```
